512 devices in a mesh: dp: 64 (over x, z), tensor: 8 (over y, core).
Axes of the slice: x: 4, y: 4, z: 16, core: 2. Of those that a mesh axis runs over, the one named last changes fastest.
Arguments:
- acts: bfloat16 [128, 4, 64, 4096], P('dp', None, None, 'tensor'), may hold values from -6 to 6
- noise_draws: bfloat16 [128, 4, 64, 2048], P('dp', None, None, 'tensor'), may hold values from -6 to 6
- times: float32 [128, 4], P('dp'), may hold values from 0 to 1
- cond: int32 [128, 16], P('dp'), may hold values from 0 to 1023
- emb: bfloat16 [1024, 2048], P(None, 'tensor'), may hold values from -1.5 to 1.5
- weight: bfloat16 [4096, 2048], P('dp', 'tensor'), may hold values from -0.09375 to 0.09375
- noise: float32 [4096, 2048], P('dp', 'tensor'), may hold values from -6 to 6
Outputs:
- clipped_sum: float32 [4096, 2048], P('dp', 'tensor')
- update: float32 [4096, 2048], P('dp', 'tensor')
- norms: float32 [128], P('dp')
The draws below stay inside these ranges and needn't reach their ends.
All inputs are finite; a program needn't handle non-finite values.
Results may differ from the reference program's by a relative error of at most 0.0017.
Values may be sent and summed in bfloat16 or wider, within the bound.
No kernel may reach another device: no remote copies, remote signals or barrier semaphores. Data moves between devices by JAX's collectives and lax.ppermute only.
A program may use at most 64 MiB of HBM per device.

```python
import math
import jax
import jax.numpy as jnp
import numpy as np
from jax import lax

D = 4096
DO = 2048
VOCAB = 1024
NCOND = 16
A = 4
TW = 64
RECORDS = 128


def set_ends(entries, key, smallest, largest):
    dims = entries.shape
    spot = [jax.random.randint(jax.random.fold_in(key, axis), (), 0, dims[axis]) for axis in range(len(dims))]
    entries = entries.at[tuple(spot)].set(smallest)
    longest = dims.index(max(dims))
    spot[longest] = (spot[longest] + 1) % dims[longest]
    return entries.at[tuple(spot)].set(largest)


def shard_levels(own_key, dims, split, smallest, top_value):
    loudness, own = 1.0, jax.random.fold_in(own_key, 6)
    for position, shards_of in split:
        steps = jnp.exp(jax.random.uniform(jax.random.fold_in(own, position), (shards_of,), jnp.float32, smallest / len(split), top_value / len(split)))
        loudness = loudness * jnp.repeat(steps, dims[position] // shards_of).reshape([-1 if axis == position else 1 for axis in range(len(dims))])
    return loudness


def rank_bounds(count, slope):
    loads = [(1 << 20) // math.isqrt(grade ** slope) + 1 for grade in range(1, count + 1)]
    deviation = 1 + sum(loads) // (1 << 30)
    return np.cumsum(np.array([max(1, weight // deviation) for weight in loads]))


def skewed_ids(own_key, dims, amount, slope):
    listing = rank_bounds(amount, slope)
    lot = jax.random.randint(jax.random.fold_in(own_key, 1), dims, 0, int(listing[amount - 1]))
    grade = jnp.searchsorted(jnp.asarray(listing, jnp.int32), lot, side="right")
    return jax.random.permutation(jax.random.fold_in(own_key, 2), amount)[grade].astype(jnp.int32)


def gaussian(key, extent, deviation, reach, pieces=(), kind=jnp.bfloat16):
    values = jax.random.normal(key, extent, jnp.float32) * deviation
    if len(pieces) > 0:
        values = shard_levels(key, extent, pieces, -0.22, 0.18) * values
    return jnp.clip(values, min=-reach, max=reach).astype(kind)


def setup_inputs(seed: int = 0) -> dict:
    seeds = jax.random.split(jax.random.key(seed), 8)
    return {
        "acts": gaussian(seeds[0], (RECORDS, A, TW, D), 1.0, 6.0, ((0, 64), (3, 8))),
        "noise_draws": gaussian(seeds[1], (RECORDS, A, TW, DO), 1.0, 6.0, ((0, 64), (3, 8))),
        "times": jnp.clip(1.0 * jax.random.uniform(seeds[2], (RECORDS, A), jnp.float32) ** shard_levels(seeds[2], (RECORDS, A), ((0, 64),), -0.2, 0.2), 0.0, 1.0),
        "cond": set_ends(skewed_ids(seeds[3], (RECORDS, NCOND), VOCAB, 2), jax.random.fold_in(seeds[3], 3), 0, VOCAB - 1).astype(jnp.int32),
        "emb": gaussian(seeds[4], (VOCAB, DO), NCOND ** -0.5, 1.5, ((1, 8),)),
        "weight": gaussian(seeds[5], (D, DO), D ** -0.5, 0.09375, ((0, 64), (1, 8))),
        "noise": gaussian(seeds[6], (D, DO), 1.0, 6.0, ((0, 64), (1, 8)), jnp.float32),
    }


def reference(acts, noise_draws, times, cond, emb, weight, noise):
    rows_rec = A * TW
    vocab_ids = jnp.arange(VOCAB, dtype=jnp.int32)
    counts = lax.optimization_barrier(jnp.sum((cond[:, :, None] == vocab_ids[None, None, :]).astype(jnp.float32), axis=1)).astype(jnp.bfloat16)
    bias = jnp.dot(counts, emb, preferred_element_type=jnp.float32)
    weights_t = 1.0 / (times + 0.25)
    scale = 1.0 / math.sqrt(A * TW)
    bound = 2.0 * math.sqrt(D * DO)

    def record(inputs):
        h_four, e_four, brow, wrec = inputs
        hflat = h_four.reshape(rows_rec, D)
        pred = jnp.dot(hflat, weight, preferred_element_type=jnp.float32) + brow[None, :]
        wrow = jnp.repeat(wrec, TW)[:, None]
        grads = (wrow * (pred - e_four.reshape(rows_rec, DO).astype(jnp.float32)) * scale).astype(jnp.bfloat16)
        gram_h = jnp.dot(hflat, hflat.T, preferred_element_type=jnp.float32)
        gram_g = jnp.dot(grads, grads.T, preferred_element_type=jnp.float32)
        return (jnp.sum(gram_h * gram_g), grads)
    squares, all_grads = lax.map(record, (acts, noise_draws, bias, weights_t))
    norms = jnp.sqrt(squares)
    clip = bound / jnp.maximum(norms, bound)

    def accumulate(total, inputs):
        h_four, grads, factor = inputs
        hflat = h_four.reshape(rows_rec, D)
        return (total + factor * jnp.dot(hflat.T, grads, preferred_element_type=jnp.float32), None)
    clipped_sum, _ = lax.scan(accumulate, jnp.zeros((D, DO), jnp.float32), (acts, all_grads, clip))
    update = (clipped_sum + bound * noise) / RECORDS
    return (clipped_sum, update, norms)
```

```python
import functools
import math

import jax
import jax.numpy as jnp
from jax import lax
from jax.experimental import pallas as pl
from jax.experimental.pallas import tpu as pltpu
from jax.sharding import Mesh, PartitionSpec as P

D = 4096
DO = 2048
F32 = jnp.float32
BF16 = jnp.bfloat16
VMEM_LIMIT = 40 * 1024 * 1024


def params(**kw):
    return pltpu.CompilerParams(vmem_limit_bytes=VMEM_LIMIT, **kw)


def dot(a, b, ca, cb):
    return lax.dot_general(a, b, (((ca,), (cb,)), ((), ())), preferred_element_type=F32)


def gram_kernel(h_ref, o_ref):
    @pl.when(pl.program_id(0) == 0)
    def _():
        o_ref[...] = jnp.zeros_like(o_ref)

    recs, rows, _ = o_ref.shape
    for j in range(h_ref.shape[0]):
        for r in range(recs):
            h = h_ref[j, r * rows : (r + 1) * rows, :]
            o_ref[r] += dot(h, h, 1, 1)


def grad_kernel(h_ref, w_ref, n_ref, b_ref, t_ref, gh_ref, g_ref, sq_ref, acc):
    i = pl.program_id(0)
    blocks = h_ref.shape[0]
    feats = h_ref.shape[2]
    part = dot(h_ref[0], w_ref[0:feats, :], 1, 0)
    for j in range(1, blocks):
        part += dot(h_ref[j], w_ref[j * feats : (j + 1) * feats, :], 1, 0)

    @pl.when(i == 0)
    def _():
        acc[...] = part

    @pl.when(i > 0)
    def _():
        acc[...] += part

    @pl.when(i == pl.num_programs(0) - 1)
    def _():
        recs, rows, _ = gh_ref.shape
        lane = lax.broadcasted_iota(jnp.int32, sq_ref.shape, 1)
        out = jnp.zeros(sq_ref.shape, F32)
        for r in range(recs):
            at = slice(r * rows, (r + 1) * rows)
            pred = acc[at, :] + b_ref[r : r + 1, :]
            g = (t_ref[at, :] * (pred - n_ref[at, :].astype(F32))).astype(BF16)
            g_ref[at, :] = g
            out = jnp.where(lane == r, jnp.sum(gh_ref[r] * dot(g, g, 1, 1)), out)
        sq_ref[...] = out


def sum_kernel(sq_ref, h_ref, g_ref, c_ref, *, bound, recs):
    rows = g_ref.shape[0] // recs
    feats = h_ref.shape[2]
    norms = jnp.sqrt(jnp.sum(sq_ref[...], axis=0, keepdims=True))
    clip = bound / jnp.maximum(norms, bound)
    for j in range(h_ref.shape[0]):
        total = None
        for r in range(recs):
            at = slice(r * rows, (r + 1) * rows)
            block = dot(h_ref[j, at, :], g_ref[at, :], 0, 0) * clip[0:1, r : r + 1]
            total = block if total is None else total + block
        c_ref[j * feats : (j + 1) * feats, :] = total.astype(BF16)


def add_kernel(x_ref, o_ref):
    step = 128

    @pl.loop(0, o_ref.shape[0] // step)
    def _(i):
        at = pl.ds(pl.multiple_of(i * step, step), step)
        total = x_ref[0, at, :].astype(F32)
        for k in range(1, x_ref.shape[0]):
            total += x_ref[k, at, :].astype(F32)
        o_ref[at, :] = total.astype(o_ref.dtype)


def gather(v, axis):
    n = lax.axis_size(axis)
    return lax.all_to_all(jnp.broadcast_to(v[None], (n,) + v.shape), axis, 0, 0)


def on_device(acts, noise_draws, times, cond, emb, weight, noise):
    recs, draws, events, feats = acts.shape
    rows = draws * events
    local_out = weight.shape[1]
    tensor = ("y", "core")
    nt = lax.axis_size("y") * lax.axis_size("core")
    nx, nz = lax.axis_size("x"), lax.axis_size("z")
    bound = 2.0 * math.sqrt(D * DO)

    full = lax.all_gather(acts.reshape(recs * rows, feats), tensor, axis=0, tiled=False)

    wz = gather(weight, "z").reshape(nz * weight.shape[0], local_out)
    wfull = gather(wz, "x").reshape(D, local_out)

    vocab_ids = lax.broadcasted_iota(jnp.int32, (1, 1, emb.shape[0]), 2)
    counts = jnp.sum((cond[:, :, None] == vocab_ids).astype(F32), axis=1).astype(BF16)
    bias = jnp.dot(counts, emb, preferred_element_type=F32)
    wrow = jnp.repeat(
        (1.0 / (times + 0.25)).reshape(recs * draws) * (1.0 / math.sqrt(rows)), events
    )[:, None]

    step = 2
    grid = nt // step
    h_spec = pl.BlockSpec((step, recs * rows, feats), lambda i: (i, 0, 0))
    whole = lambda *shape: pl.BlockSpec(shape, lambda i: (0,) * len(shape))
    gram_h = pl.pallas_call(
        gram_kernel,
        grid=(grid,),
        in_specs=[h_spec],
        out_specs=whole(recs, rows, rows),
        out_shape=jax.ShapeDtypeStruct((recs, rows, rows), F32),
        compiler_params=params(),
        cost_estimate=pl.CostEstimate(
            flops=2 * recs * rows * rows * D, bytes_accessed=2 * recs * rows * D, transcendentals=0
        ),
    )(full)
    grads, sq = pl.pallas_call(
        grad_kernel,
        grid=(grid,),
        in_specs=[
            h_spec,
            pl.BlockSpec((step * feats, local_out), lambda i: (i, 0)),
            whole(recs * rows, local_out),
            whole(recs, local_out),
            whole(recs * rows, 1),
            whole(recs, rows, rows),
        ],
        out_specs=[whole(recs * rows, local_out), whole(nt, 128)],
        out_shape=[
            jax.ShapeDtypeStruct((recs * rows, local_out), BF16),
            jax.ShapeDtypeStruct((nt, 128), F32),
        ],
        scratch_shapes=[pltpu.VMEM((recs * rows, local_out), F32)],
        compiler_params=params(),
        cost_estimate=pl.CostEstimate(
            flops=2 * recs * rows * local_out * D,
            bytes_accessed=2 * recs * rows * D + 2 * D * local_out,
            transcendentals=0,
        ),
    )(full, wfull, noise_draws.reshape(recs * rows, local_out), bias, wrow, gram_h)

    sq_all = lax.all_to_all(sq.reshape(nt, 1, 128), tensor, 0, 0).reshape(nt, 128)
    norms = jnp.sqrt(jnp.sum(sq_all[:, :recs], axis=0))

    partial = pl.pallas_call(
        functools.partial(sum_kernel, bound=bound, recs=recs),
        grid=(grid,),
        in_specs=[whole(nt, 128), h_spec, whole(recs * rows, local_out)],
        out_specs=pl.BlockSpec((step * feats, local_out), lambda i: (i, 0)),
        out_shape=jax.ShapeDtypeStruct((D, local_out), BF16),
        compiler_params=params(),
        cost_estimate=pl.CostEstimate(
            flops=2 * recs * rows * local_out * D,
            bytes_accessed=2 * recs * rows * D + 2 * D * local_out,
            transcendentals=0,
        ),
    )(sq_all, full, grads)

    over_x = lax.all_to_all(partial.reshape(nx, D // nx, local_out), "x", 0, 0)
    sum_x = pl.pallas_call(
        add_kernel,
        out_shape=jax.ShapeDtypeStruct((D // nx, local_out), BF16),
        compiler_params=params(),
    )(over_x)
    over_z = lax.all_to_all(sum_x.reshape(nz, D // nx // nz, local_out), "z", 0, 0)
    clipped_sum = jnp.sum(over_z.astype(F32), axis=0)
    total_recs = recs * nx * nz
    update = (clipped_sum + bound * noise) / total_recs
    return (clipped_sum, update, norms)


def solution(mesh):
    grid = Mesh(mesh.devices.reshape(4, 16, 4, 2), ("x", "z", "y", "core"))
    dp, tensor = ("x", "z"), ("y", "core")
    in_specs = (
        P(dp, None, None, tensor),
        P(dp, None, None, tensor),
        P(dp, None),
        P(dp, None),
        P(None, tensor),
        P(dp, tensor),
        P(dp, tensor),
    )
    out_specs = (P(dp, tensor), P(dp, tensor), P(dp))
    return jax.shard_map(
        on_device, mesh=grid, in_specs=in_specs, out_specs=out_specs, check_vma=False
    )
```

```python
import functools
import math

import jax
import jax.numpy as jnp
from jax import lax
from jax.experimental import pallas as pl
from jax.experimental.pallas import tpu as pltpu
from jax.sharding import Mesh, PartitionSpec as P

D = 4096
DO = 2048
F32 = jnp.float32
BF16 = jnp.bfloat16
F16 = jnp.float16
SCALE = 256.0
VMEM_LIMIT = 60 * 1024 * 1024


def params(**kw):
    return pltpu.CompilerParams(vmem_limit_bytes=VMEM_LIMIT, **kw)


def dot(a, b, ca, cb):
    return lax.dot_general(a, b, (((ca,), (cb,)), ((), ())), preferred_element_type=F32)


def gram_kernel(h_ref, o_ref):
    @pl.when(pl.program_id(0) == 0)
    def _():
        o_ref[...] = jnp.zeros_like(o_ref)

    recs, rows, _ = o_ref.shape
    for j in range(h_ref.shape[0]):
        for r in range(recs):
            h = h_ref[j, r * rows : (r + 1) * rows, :]
            o_ref[r] += dot(h, h, 1, 1)


def grad_kernel(h_ref, w_ref, n_ref, b_ref, t_ref, gh_ref, g_ref, sq_ref, acc):
    i = pl.program_id(0)
    blocks = h_ref.shape[0]
    feats = h_ref.shape[2]
    part = dot(h_ref[0], w_ref[0:feats, :], 1, 0)
    for j in range(1, blocks):
        part += dot(h_ref[j], w_ref[j * feats : (j + 1) * feats, :], 1, 0)

    @pl.when(i == 0)
    def _():
        acc[...] = part

    @pl.when(i > 0)
    def _():
        acc[...] += part

    @pl.when(i == pl.num_programs(0) - 1)
    def _():
        recs, rows, _ = gh_ref.shape
        lane = lax.broadcasted_iota(jnp.int32, sq_ref.shape, 1)
        out = jnp.zeros(sq_ref.shape, F32)
        for r in range(recs):
            at = slice(r * rows, (r + 1) * rows)
            pred = acc[at, :] + b_ref[r : r + 1, :]
            g = (t_ref[at, :] * (pred - n_ref[at, :].astype(F32))).astype(BF16)
            g_ref[at, :] = g
            out = jnp.where(lane == r, jnp.sum(gh_ref[r] * dot(g, g, 1, 1)), out)
        sq_ref[...] = out


def sum_kernel(sq_ref, h_ref, g_ref, c_ref, *, bound, recs):
    rows = g_ref.shape[0] // recs
    feats = h_ref.shape[2]
    norms = jnp.sqrt(jnp.sum(sq_ref[...], axis=0, keepdims=True))
    clip = bound / jnp.maximum(norms, bound)
    for j in range(h_ref.shape[0]):
        total = None
        for r in range(recs):
            at = slice(r * rows, (r + 1) * rows)
            block = dot(h_ref[j, at, :], g_ref[at, :], 0, 0) * clip[0:1, r : r + 1]
            total = block if total is None else total + block
        c_ref[j * feats : (j + 1) * feats, :] = root(total)


def root(v):
    return v * lax.rsqrt(jnp.maximum(jnp.abs(v), 1e-30)) * SCALE


def unroot(v):
    v = v.astype(F32)
    return v * jnp.abs(v) * (1.0 / (SCALE * SCALE))


def gather(v, axis):
    n = lax.axis_size(axis)
    return lax.all_to_all(jnp.broadcast_to(v[None], (n,) + v.shape), axis, 0, 0)


def on_device(acts, noise_draws, times, cond, emb, weight, noise):
    recs, draws, events, feats = acts.shape
    rows = draws * events
    local_out = weight.shape[1]
    tensor = ("y", "core")
    nt = lax.axis_size("y") * lax.axis_size("core")
    nx, nz = lax.axis_size("x"), lax.axis_size("z")
    bound = 2.0 * math.sqrt(D * DO)

    full = lax.all_gather(acts.reshape(recs * rows, feats), tensor, axis=0, tiled=False)

    wz = gather(weight, "z").reshape(nz * weight.shape[0], local_out)
    wfull = gather(wz, "x").reshape(D, local_out)

    vocab_ids = lax.broadcasted_iota(jnp.int32, (1, 1, emb.shape[0]), 2)
    counts = jnp.sum((cond[:, :, None] == vocab_ids).astype(F32), axis=1).astype(BF16)
    bias = jnp.dot(counts, emb, preferred_element_type=F32)
    wrow = jnp.repeat(
        (1.0 / (times + 0.25)).reshape(recs * draws) * (1.0 / math.sqrt(rows)), events
    )[:, None]

    step = 2
    grid = nt // step
    h_spec = pl.BlockSpec((step, recs * rows, feats), lambda i: (i, 0, 0))
    whole = lambda *shape: pl.BlockSpec(shape, lambda i: (0,) * len(shape))
    gram_h = pl.pallas_call(
        gram_kernel,
        grid=(grid,),
        in_specs=[h_spec],
        out_specs=whole(recs, rows, rows),
        out_shape=jax.ShapeDtypeStruct((recs, rows, rows), F32),
        compiler_params=params(),
        cost_estimate=pl.CostEstimate(
            flops=2 * recs * rows * rows * D, bytes_accessed=2 * recs * rows * D, transcendentals=0
        ),
    )(full)
    grads, sq = pl.pallas_call(
        grad_kernel,
        grid=(grid,),
        in_specs=[
            h_spec,
            pl.BlockSpec((step * feats, local_out), lambda i: (i, 0)),
            whole(recs * rows, local_out),
            whole(recs, local_out),
            whole(recs * rows, 1),
            whole(recs, rows, rows),
        ],
        out_specs=[whole(recs * rows, local_out), whole(nt, 128)],
        out_shape=[
            jax.ShapeDtypeStruct((recs * rows, local_out), BF16),
            jax.ShapeDtypeStruct((nt, 128), F32),
        ],
        scratch_shapes=[pltpu.VMEM((recs * rows, local_out), F32)],
        compiler_params=params(),
        cost_estimate=pl.CostEstimate(
            flops=2 * recs * rows * local_out * D,
            bytes_accessed=2 * recs * rows * D + 2 * D * local_out,
            transcendentals=0,
        ),
    )(full, wfull, noise_draws.reshape(recs * rows, local_out), bias, wrow, gram_h)

    sq_all = lax.all_to_all(sq.reshape(nt, 1, 128), tensor, 0, 0).reshape(nt, 128)
    norms = jnp.sqrt(jnp.sum(sq_all[:, :recs], axis=0))

    partial = pl.pallas_call(
        functools.partial(sum_kernel, bound=bound, recs=recs),
        grid=(grid,),
        in_specs=[whole(nt, 128), h_spec, whole(recs * rows, local_out)],
        out_specs=pl.BlockSpec((step * feats, local_out), lambda i: (i, 0)),
        out_shape=jax.ShapeDtypeStruct((D, local_out), F32),
        compiler_params=params(),
        cost_estimate=pl.CostEstimate(
            flops=2 * recs * rows * local_out * D,
            bytes_accessed=2 * recs * rows * D + 2 * D * local_out,
            transcendentals=0,
        ),
    )(sq_all, full, grads)

    sent = partial.astype(F16).reshape(nx, D // nx, local_out)
    sum_x = jnp.sum(unroot(lax.all_to_all(sent, "x", 0, 0)), axis=0)
    sent = root(sum_x).astype(F16).reshape(nz, D // nx // nz, local_out)
    clipped_sum = jnp.sum(unroot(lax.all_to_all(sent, "z", 0, 0)), axis=0)
    total_recs = recs * nx * nz
    update = (clipped_sum + bound * noise) / total_recs
    return (clipped_sum, update, norms)


def solution(mesh):
    grid = Mesh(mesh.devices.reshape(4, 16, 4, 2), ("x", "z", "y", "core"))
    dp, tensor = ("x", "z"), ("y", "core")
    in_specs = (
        P(dp, None, None, tensor),
        P(dp, None, None, tensor),
        P(dp, None),
        P(dp, None),
        P(None, tensor),
        P(dp, tensor),
        P(dp, tensor),
    )
    out_specs = (P(dp, tensor), P(dp, tensor), P(dp))
    return jax.shard_map(
        on_device, mesh=grid, in_specs=in_specs, out_specs=out_specs, check_vma=False
    )
```

```python
import functools
import math

import jax
import jax.numpy as jnp
from jax import lax
from jax.experimental import pallas as pl
from jax.experimental.pallas import tpu as pltpu
from jax.sharding import Mesh, PartitionSpec as P

D = 4096
DO = 2048
F32 = jnp.float32
BF16 = jnp.bfloat16
F16 = jnp.float16
SCALE = 256.0
TAIL = 16
VMEM_LIMIT = 40 * 1024 * 1024


def params(**kw):
    return pltpu.CompilerParams(vmem_limit_bytes=VMEM_LIMIT, **kw)


def dot(a, b, ca, cb):
    return lax.dot_general(a, b, (((ca,), (cb,)), ((), ())), preferred_element_type=F32)


def gram_kernel(h_ref, o_ref):
    @pl.when(pl.program_id(0) == 0)
    def _():
        o_ref[...] = jnp.zeros_like(o_ref)

    recs, rows, _ = o_ref.shape
    for j in range(h_ref.shape[0]):
        for r in range(recs):
            h = h_ref[j, r * rows : (r + 1) * rows, :]
            o_ref[r] += dot(h, h, 1, 1)


def grad_kernel(h_ref, w_ref, n_ref, b_ref, t_ref, gh_ref, g_ref, sq_ref, acc):
    i = pl.program_id(0)
    blocks = h_ref.shape[0]
    feats = h_ref.shape[2]
    part = dot(h_ref[0], w_ref[0:feats, :], 1, 0)
    for j in range(1, blocks):
        part += dot(h_ref[j], w_ref[j * feats : (j + 1) * feats, :], 1, 0)

    @pl.when(i == 0)
    def _():
        acc[...] = part

    @pl.when(i > 0)
    def _():
        acc[...] += part

    @pl.when(i == pl.num_programs(0) - 1)
    def _():
        recs, rows, _ = gh_ref.shape
        lane = lax.broadcasted_iota(jnp.int32, sq_ref.shape, 1)
        out = jnp.zeros(sq_ref.shape, F32)
        for r in range(recs):
            at = slice(r * rows, (r + 1) * rows)
            pred = acc[at, :] + b_ref[r : r + 1, :]
            g = (t_ref[at, :] * (pred - n_ref[at, :].astype(F32))).astype(BF16)
            g_ref[at, :] = g
            out = jnp.where(lane == r, jnp.sum(gh_ref[r] * dot(g, g, 1, 1)), out)
        sq_ref[...] = out


def pack_kernel(sq_ref, g_ref, o_ref, *, bound):
    rows = g_ref.shape[0]
    norms = jnp.sqrt(jnp.sum(sq_ref[...], axis=0, keepdims=True))
    clip = bound / jnp.maximum(norms, bound)
    high = clip.astype(BF16).astype(F32)
    mid = (clip - high).astype(BF16).astype(F32)
    low = clip - high - mid
    shape = (TAIL, clip.shape[1])
    row = lax.broadcasted_iota(jnp.int32, shape, 0)
    tail = jnp.zeros(shape, F32)
    for k, term in enumerate((high, mid, low)):
        tail = jnp.where(row == k, jnp.broadcast_to(term, shape), tail)
    tail = jnp.concatenate([tail] * (o_ref.shape[2] // clip.shape[1]), axis=1).astype(BF16)
    for k in range(o_ref.shape[0]):
        o_ref[k, 0:rows, :] = g_ref[...]
        o_ref[k, rows : rows + TAIL, :] = tail


def sum_kernel(h_ref, g_ref, c_ref, *, recs):
    i = pl.program_id(0)
    rows = (g_ref.shape[1] - TAIL) // recs
    feats = h_ref.shape[2]
    tail = g_ref[0, recs * rows : recs * rows + TAIL, :].astype(F32)
    clip = jnp.sum(tail, axis=0, keepdims=True)
    for j in range(h_ref.shape[0]):
        total = None
        for r in range(recs):
            at = slice(r * rows, (r + 1) * rows)
            block = dot(h_ref[j, at, :], g_ref[0, at, :], 0, 0) * clip[0:1, r : r + 1]
            total = block if total is None else total + block
        out = slice(j * feats, (j + 1) * feats)

        @pl.when(i == 0)
        def _():
            c_ref[out, :] = total

        @pl.when(i > 0)
        def _():
            c_ref[out, :] += total


def root(v):
    return v * lax.rsqrt(jnp.maximum(jnp.abs(v), 1e-30)) * SCALE


def unroot(v):
    v = v.astype(F32)
    return v * jnp.abs(v) * (1.0 / (SCALE * SCALE))


def gather(v, axis):
    n = lax.axis_size(axis)
    return lax.all_to_all(jnp.broadcast_to(v[None], (n,) + v.shape), axis, 0, 0)


def on_device(acts, noise_draws, times, cond, emb, weight, noise):
    recs, draws, events, feats = acts.shape
    rows = draws * events
    local_out = weight.shape[1]
    tensor = ("y", "core")
    nt = lax.axis_size("y") * lax.axis_size("core")
    nx, nz = lax.axis_size("x"), lax.axis_size("z")
    bound = 2.0 * math.sqrt(D * DO)

    own = acts.reshape(recs * rows, feats)
    full = lax.all_gather(own, tensor, axis=0, tiled=False)
    swap = [(a * nx + b, b * nx + a) for a in range(nx) for b in range(nx)]
    swapped = lax.ppermute(own, ("x", "y"), swap)

    wz = gather(weight, "z").reshape(nz * weight.shape[0], local_out)
    swapped, wz = lax.optimization_barrier((swapped, wz))
    mine = lax.all_gather(swapped, tensor, axis=0, tiled=False)
    wfull = gather(wz, "x").reshape(D, local_out)

    vocab_ids = lax.broadcasted_iota(jnp.int32, (1, 1, emb.shape[0]), 2)
    counts = jnp.sum((cond[:, :, None] == vocab_ids).astype(F32), axis=1).astype(BF16)
    bias = jnp.dot(counts, emb, preferred_element_type=F32)
    wrow = jnp.repeat(
        (1.0 / (times + 0.25)).reshape(recs * draws) * (1.0 / math.sqrt(rows)), events
    )[:, None]

    step = 2
    grid = nt // step
    h_spec = pl.BlockSpec((step, recs * rows, feats), lambda i: (i, 0, 0))
    whole = lambda *shape: pl.BlockSpec(shape, lambda i: (0,) * len(shape))
    gram_h = pl.pallas_call(
        gram_kernel,
        grid=(grid,),
        in_specs=[h_spec],
        out_specs=whole(recs, rows, rows),
        out_shape=jax.ShapeDtypeStruct((recs, rows, rows), F32),
        compiler_params=params(),
        cost_estimate=pl.CostEstimate(
            flops=2 * recs * rows * rows * D, bytes_accessed=2 * recs * rows * D, transcendentals=0
        ),
    )(full)
    grads, sq = pl.pallas_call(
        grad_kernel,
        grid=(grid,),
        in_specs=[
            h_spec,
            pl.BlockSpec((step * feats, local_out), lambda i: (i, 0)),
            whole(recs * rows, local_out),
            whole(recs, local_out),
            whole(recs * rows, 1),
            whole(recs, rows, rows),
        ],
        out_specs=[whole(recs * rows, local_out), whole(nt, 128)],
        out_shape=[
            jax.ShapeDtypeStruct((recs * rows, local_out), BF16),
            jax.ShapeDtypeStruct((nt, 128), F32),
        ],
        scratch_shapes=[pltpu.VMEM((recs * rows, local_out), F32)],
        compiler_params=params(),
        cost_estimate=pl.CostEstimate(
            flops=2 * recs * rows * local_out * D,
            bytes_accessed=2 * recs * rows * D + 2 * D * local_out,
            transcendentals=0,
        ),
    )(full, wfull, noise_draws.reshape(recs * rows, local_out), bias, wrow, gram_h)

    sq_all = lax.all_to_all(sq.reshape(nt, 1, 128), tensor, 0, 0).reshape(nt, 128)
    norms = jnp.sqrt(jnp.sum(sq_all[:, :recs], axis=0))

    packed = pl.pallas_call(
        functools.partial(pack_kernel, bound=bound),
        out_shape=jax.ShapeDtypeStruct((nx, recs * rows + TAIL, local_out), BF16),
        compiler_params=params(),
    )(sq_all, grads)
    packed = lax.all_to_all(packed, "x", 0, 0)
    here = pl.pallas_call(
        functools.partial(sum_kernel, recs=recs),
        grid=(nx,),
        in_specs=[
            pl.BlockSpec((nt // nx, recs * rows, feats), lambda i: (i, 0, 0)),
            pl.BlockSpec((1, recs * rows + TAIL, local_out), lambda i: (i, 0, 0)),
        ],
        out_specs=whole(D // nx, local_out),
        out_shape=jax.ShapeDtypeStruct((D // nx, local_out), F32),
        compiler_params=params(),
        cost_estimate=pl.CostEstimate(
            flops=2 * recs * rows * local_out * D,
            bytes_accessed=2 * recs * rows * (D + nx * local_out) + 4 * D // nx * local_out,
            transcendentals=0,
        ),
    )(mine, packed)

    sent = root(here).astype(F16).reshape(nz, D // nx // nz, local_out)
    clipped_sum = jnp.sum(unroot(lax.all_to_all(sent, "z", 0, 0)), axis=0)
    total_recs = recs * nx * nz
    update = (clipped_sum + bound * noise) / total_recs
    return (clipped_sum, update, norms)


def solution(mesh):
    grid = Mesh(mesh.devices.reshape(4, 16, 4, 2), ("x", "z", "y", "core"))
    dp, tensor = ("x", "z"), ("y", "core")
    in_specs = (
        P(dp, None, None, tensor),
        P(dp, None, None, tensor),
        P(dp, None),
        P(dp, None),
        P(None, tensor),
        P(dp, tensor),
        P(dp, tensor),
    )
    out_specs = (P(dp, tensor), P(dp, tensor), P(dp))
    return jax.shard_map(
        on_device, mesh=grid, in_specs=in_specs, out_specs=out_specs, check_vma=False
    )
```

```python
import functools
import math

import jax
import jax.numpy as jnp
from jax import lax
from jax.experimental import pallas as pl
from jax.experimental.pallas import tpu as pltpu
from jax.sharding import Mesh, PartitionSpec as P

D = 4096
DO = 2048
F32 = jnp.float32
BF16 = jnp.bfloat16
F16 = jnp.float16
SCALE = 256.0
TAIL = 16
MIB = 1024 * 1024


def params(mib=40):
    return pltpu.CompilerParams(vmem_limit_bytes=mib * MIB)


def dot(a, b, ca, cb):
    return lax.dot_general(a, b, (((ca,), (cb,)), ((), ())), preferred_element_type=F32)


def gram_kernel(h_ref, o_ref):
    @pl.when(pl.program_id(0) == 0)
    def _():
        o_ref[...] = jnp.zeros_like(o_ref)

    recs, rows, _ = o_ref.shape
    for j in range(h_ref.shape[0]):
        for r in range(recs):
            h = h_ref[j, r * rows : (r + 1) * rows, :]
            o_ref[r] += dot(h, h, 1, 1)


def fetch(src, dst, sems):
    copies = [pltpu.make_async_copy(src.at[j], dst.at[j], sems.at[j]) for j in range(dst.shape[0])]
    for copy in copies:
        copy.start()
    return copies


def grad_kernel(h_hbm, w_ref, n_hbm, b_ref, t_ref, gh_ref, g_ref, sq_ref, h_buf, n_buf, acc, h_sems, n_sems):
    blocks, _, feats = h_buf.shape
    h_copies = fetch(h_hbm, h_buf, h_sems)
    n_copies = fetch(n_hbm, n_buf, n_sems)
    for j in range(blocks):
        h_copies[j].wait()
        part = dot(h_buf[j], w_ref[j * feats : (j + 1) * feats, :], 1, 0)
        if j == 0:
            acc[...] = part
        else:
            acc[...] += part

    recs, rows, _ = gh_ref.shape
    lane = lax.broadcasted_iota(jnp.int32, sq_ref.shape, 1)
    out = jnp.zeros(sq_ref.shape, F32)
    for r in range(recs):
        at = slice(r * rows, (r + 1) * rows)
        n_copies[r].wait()
        pred = acc[at, :] + b_ref[r : r + 1, :]
        g = (t_ref[at, :] * (pred - n_buf[r].astype(F32))).astype(BF16)
        g_ref[at, :] = g
        out = jnp.where(lane == r, jnp.sum(gh_ref[r] * dot(g, g, 1, 1)), out)
    sq_ref[...] = out


def pack_kernel(sq_ref, g_ref, o_ref, *, bound):
    rows = g_ref.shape[0]
    norms = jnp.sqrt(jnp.sum(sq_ref[...], axis=0, keepdims=True))
    clip = bound / jnp.maximum(norms, bound)
    high = clip.astype(BF16).astype(F32)
    mid = (clip - high).astype(BF16).astype(F32)
    low = clip - high - mid
    shape = (TAIL, clip.shape[1])
    row = lax.broadcasted_iota(jnp.int32, shape, 0)
    tail = jnp.zeros(shape, F32)
    for k, term in enumerate((high, mid, low)):
        tail = jnp.where(row == k, jnp.broadcast_to(term, shape), tail)
    tail = jnp.concatenate([tail] * (o_ref.shape[2] // clip.shape[1]), axis=1).astype(BF16)
    for k in range(o_ref.shape[0]):
        o_ref[k, 0:rows, :] = g_ref[...]
        o_ref[k, rows : rows + TAIL, :] = tail


def sum_kernel(h_hbm, g_ref, c_ref, h_buf, acc, sems, *, recs):
    copies = fetch(h_hbm, h_buf, sems)
    blocks, total_rows, feats = h_buf.shape
    nx = g_ref.shape[0]
    rows = total_rows // recs
    per = blocks // nx
    for x in range(nx):
        tail = g_ref[x, total_rows : total_rows + TAIL, :].astype(F32)
        clip = jnp.sum(tail, axis=0, keepdims=True)
        for j in range(per):
            copies[x * per + j].wait()
            total = None
            for r in range(recs):
                at = slice(r * rows, (r + 1) * rows)
                block = dot(h_buf[x * per + j, at, :], g_ref[x, at, :], 0, 0) * clip[0:1, r : r + 1]
                total = block if total is None else total + block
            out = slice(j * feats, (j + 1) * feats)
            if x == 0:
                acc[out, :] = total
            else:
                acc[out, :] += total
    zl, zh, size, _ = c_ref.shape
    for b in range(zl):
        for a in range(zh):
            at = (a * zl + b) * size
            c_ref[b, a] = acc[at : at + size, :]


def root(v):
    return v * lax.rsqrt(jnp.maximum(jnp.abs(v), 1e-30)) * SCALE


def unroot(v):
    v = v.astype(F32)
    return v * jnp.abs(v) * (1.0 / (SCALE * SCALE))


def gather(v, axis):
    n = lax.axis_size(axis)
    return lax.all_to_all(jnp.broadcast_to(v[None], (n,) + v.shape), axis, 0, 0)


def on_device(acts, noise_draws, times, cond, emb, weight, noise):
    recs, draws, events, feats = acts.shape
    rows = draws * events
    local_out = weight.shape[1]
    tensor = ("y", "core")
    nt = lax.axis_size("y") * lax.axis_size("core")
    nx, nh, nl = lax.axis_size("x"), lax.axis_size("zh"), lax.axis_size("zl")
    nz = nh * nl
    bound = 2.0 * math.sqrt(D * DO)

    own = acts.reshape(recs * rows, feats)
    full = lax.all_gather(own, tensor, axis=0, tiled=False)
    swap = [(a * nx + b, b * nx + a) for a in range(nx) for b in range(nx)]
    swapped = lax.ppermute(own, ("x", "y"), swap)

    wz = lax.all_gather(weight, ("zh", "zl"), axis=0, tiled=True)
    swapped, wz = lax.optimization_barrier((swapped, wz))
    mine = lax.all_gather(swapped, tensor, axis=0, tiled=False)
    wfull = gather(wz, "x").reshape(D, local_out)

    vocab_ids = lax.broadcasted_iota(jnp.int32, (1, 1, emb.shape[0]), 2)
    counts = jnp.sum((cond[:, :, None] == vocab_ids).astype(F32), axis=1).astype(BF16)
    bias = jnp.dot(counts, emb, preferred_element_type=F32)
    wrow = jnp.repeat(
        (1.0 / (times + 0.25)).reshape(recs * draws) * (1.0 / math.sqrt(rows)), events
    )[:, None]

    step = 2
    grid = nt // step
    h_spec = pl.BlockSpec((step, recs * rows, feats), lambda i: (i, 0, 0))
    whole = lambda *shape: pl.BlockSpec(shape, lambda i: (0,) * len(shape))
    gram_h = pl.pallas_call(
        gram_kernel,
        grid=(grid,),
        in_specs=[h_spec],
        out_specs=whole(recs, rows, rows),
        out_shape=jax.ShapeDtypeStruct((recs, rows, rows), F32),
        compiler_params=params(),
        cost_estimate=pl.CostEstimate(
            flops=2 * recs * rows * rows * D, bytes_accessed=2 * recs * rows * D, transcendentals=0
        ),
    )(full)
    vmem = pl.BlockSpec(memory_space=pltpu.VMEM)
    hbm = pl.BlockSpec(memory_space=pltpu.HBM)
    grads, sq = pl.pallas_call(
        grad_kernel,
        in_specs=[hbm, vmem, hbm, vmem, vmem, vmem],
        out_specs=[vmem, vmem],
        out_shape=[
            jax.ShapeDtypeStruct((recs * rows, local_out), BF16),
            jax.ShapeDtypeStruct((nt, 128), F32),
        ],
        scratch_shapes=[
            pltpu.VMEM((nt, recs * rows, feats), BF16),
            pltpu.VMEM((recs, rows, local_out), BF16),
            pltpu.VMEM((recs * rows, local_out), F32),
            pltpu.SemaphoreType.DMA((nt,)),
            pltpu.SemaphoreType.DMA((recs,)),
        ],
        compiler_params=params(51),
        cost_estimate=pl.CostEstimate(
            flops=2 * recs * rows * local_out * D,
            bytes_accessed=2 * recs * rows * D + 2 * D * local_out,
            transcendentals=0,
        ),
    )(full, wfull, noise_draws.reshape(recs, rows, local_out), bias, wrow, gram_h)

    sq_all = lax.all_to_all(sq.reshape(nt, 1, 128), tensor, 0, 0).reshape(nt, 128)
    norms = jnp.sqrt(jnp.sum(sq_all[:, :recs], axis=0))

    packed = pl.pallas_call(
        functools.partial(pack_kernel, bound=bound),
        out_shape=jax.ShapeDtypeStruct((nx, recs * rows + TAIL, local_out), BF16),
        compiler_params=params(),
    )(sq_all, grads)
    packed = lax.all_to_all(packed, "x", 0, 0)
    block = weight.shape[0]
    here = pl.pallas_call(
        functools.partial(sum_kernel, recs=recs),
        in_specs=[hbm, vmem],
        out_specs=vmem,
        out_shape=jax.ShapeDtypeStruct((nl, nh, block, local_out), F32),
        scratch_shapes=[
            pltpu.VMEM((nt, recs * rows, feats), BF16),
            pltpu.VMEM((D // nx, local_out), F32),
            pltpu.SemaphoreType.DMA((nt,)),
        ],
        compiler_params=params(51),
        cost_estimate=pl.CostEstimate(
            flops=2 * recs * rows * local_out * D,
            bytes_accessed=2 * recs * rows * (D + nx * local_out) + 4 * D // nx * local_out,
            transcendentals=0,
        ),
    )(mine.reshape(nt, recs * rows, feats), packed)

    sent = root(here).astype(F16)
    sum_l = jnp.sum(unroot(lax.all_to_all(sent, "zl", 0, 0)), axis=0)
    sent = root(sum_l).astype(F16)
    clipped_sum = jnp.sum(unroot(lax.all_to_all(sent, "zh", 0, 0)), axis=0)
    total_recs = recs * nx * nz
    update = (clipped_sum + bound * noise) / total_recs
    return (clipped_sum, update, norms)


def solution(mesh):
    grid = Mesh(mesh.devices.reshape(4, 4, 4, 4, 2), ("x", "zh", "zl", "y", "core"))
    dp, tensor = ("x", "zh", "zl"), ("y", "core")
    in_specs = (
        P(dp, None, None, tensor),
        P(dp, None, None, tensor),
        P(dp, None),
        P(dp, None),
        P(None, tensor),
        P(dp, tensor),
        P(dp, tensor),
    )
    out_specs = (P(dp, tensor), P(dp, tensor), P(dp))
    return jax.shard_map(
        on_device, mesh=grid, in_specs=in_specs, out_specs=out_specs, check_vma=False
    )
```

```python
import functools
import math

import jax
import jax.numpy as jnp
from jax import lax
from jax.experimental import pallas as pl
from jax.experimental.pallas import tpu as pltpu
from jax.sharding import Mesh, PartitionSpec as P

D = 4096
DO = 2048
F32 = jnp.float32
BF16 = jnp.bfloat16
F16 = jnp.float16
SCALE = 256.0
TAIL = 16
MIB = 1024 * 1024


def params(mib=40):
    return pltpu.CompilerParams(vmem_limit_bytes=mib * MIB)


def dot(a, b, ca, cb):
    return lax.dot_general(a, b, (((ca,), (cb,)), ((), ())), preferred_element_type=F32)


def fetch(src, dst, sems):
    copies = [pltpu.make_async_copy(src.at[j], dst.at[j], sems.at[j]) for j in range(dst.shape[0])]
    for copy in copies:
        copy.start()
    return copies


def grad_kernel(*refs):
    h_hbm, n_hbm, b_ref, t_ref = refs[:4]
    w_refs, (g_ref, sq_ref, h_buf, n_buf, h_sems, n_sems) = refs[4:-6], refs[-6:]
    total_rows, feats = h_buf.shape[1:]
    recs, rows, _ = n_buf.shape
    nx = len(w_refs) // 2
    h_copies = fetch(h_hbm, h_buf, h_sems)
    n_copies = fetch(n_hbm, n_buf, n_sems)
    for copy in h_copies:
        copy.wait()
    here = lax.axis_index("x")
    lane = lax.broadcasted_iota(jnp.int32, sq_ref.shape, 1)
    out = jnp.zeros(sq_ref.shape, F32)
    for r in range(recs):
        at = slice(r * rows, (r + 1) * rows)
        pred, gram = None, None
        for k, w_ref in enumerate(w_refs):
            h = h_buf[lax.rem(here + k // 2, nx) * 2 + k % 2, at, :]
            p, q = dot(h, w_ref[...], 1, 0), dot(h, h, 1, 1)
            pred = p if pred is None else pred + p
            gram = q if gram is None else gram + q
        n_copies[r].wait()
        pred = pred + b_ref[r : r + 1, :]
        g = (t_ref[at, :] * (pred - n_buf[r].astype(F32))).astype(BF16)
        g_ref[at, :] = g
        out = jnp.where(lane == r, jnp.sum(gram * dot(g, g, 1, 1)), out)
    sq_ref[...] = out


def pack_kernel(sq_ref, g_ref, o_ref, *, bound):
    rows = g_ref.shape[0]
    norms = jnp.sqrt(jnp.sum(sq_ref[...], axis=0, keepdims=True))
    clip = bound / jnp.maximum(norms, bound)
    high = clip.astype(BF16).astype(F32)
    mid = (clip - high).astype(BF16).astype(F32)
    low = clip - high - mid
    shape = (TAIL, clip.shape[1])
    row = lax.broadcasted_iota(jnp.int32, shape, 0)
    tail = jnp.zeros(shape, F32)
    for k, term in enumerate((high, mid, low)):
        tail = jnp.where(row == k, jnp.broadcast_to(term, shape), tail)
    tail = jnp.concatenate([tail] * (o_ref.shape[2] // clip.shape[1]), axis=1).astype(BF16)
    for k in range(o_ref.shape[0]):
        o_ref[k, 0:rows, :] = g_ref[...]
        o_ref[k, rows : rows + TAIL, :] = tail


def sum_kernel(h_hbm, g_ref, keep_ref, send_ref, h_buf, acc, sems, *, recs):
    copies = fetch(h_hbm, h_buf, sems)
    blocks, total_rows, feats = h_buf.shape
    nx = g_ref.shape[0]
    rows = total_rows // recs
    per = blocks // nx
    for x in range(nx):
        tail = g_ref[x, total_rows : total_rows + TAIL, :].astype(F32)
        clip = jnp.sum(tail, axis=0, keepdims=True)
        for j in range(per):
            copies[x * per + j].wait()
            total = None
            for r in range(recs):
                at = slice(r * rows, (r + 1) * rows)
                block = dot(h_buf[x * per + j, at, :], g_ref[x, at, :], 0, 0) * clip[0:1, r : r + 1]
                total = block if total is None else total + block
            out = slice(j * feats, (j + 1) * feats)
            if x == 0:
                acc[out, :] = total
            else:
                acc[out, :] += total
    groups, size, _ = keep_ref.shape
    odd = lax.axis_index("zp")
    for q in range(groups):
        keep_ref[q] = acc[pl.ds(pl.multiple_of((2 * q + odd) * size, size), size), :]
        send_ref[q] = acc[pl.ds(pl.multiple_of((2 * q + 1 - odd) * size, size), size), :]


def root(v):
    return v * lax.rsqrt(jnp.maximum(jnp.abs(v), 1e-30)) * SCALE


def unroot(v):
    v = v.astype(F32)
    return v * jnp.abs(v) * (1.0 / (SCALE * SCALE))


def ring_gather(v):
    up, down = [(i, (i + 1) % 4) for i in range(4)], [(i, (i + 3) % 4) for i in range(4)]
    half = v.shape[0] // 2
    a, b = v[:half], v[half:]
    a3, b1 = lax.ppermute(a, "x", up), lax.ppermute(b, "x", down)
    b3, a1 = lax.ppermute(b, "x", up), lax.ppermute(a, "x", down)
    a2, b2 = lax.ppermute(a3, "x", up), lax.ppermute(b1, "x", down)
    return [a, b, a1, b1, a2, b2, a3, b3]


def on_device(acts, noise_draws, times, cond, emb, weight, noise):
    recs, draws, events, feats = acts.shape
    rows = draws * events
    local_out = weight.shape[1]
    tensor = ("y", "core")
    nt = lax.axis_size("y") * lax.axis_size("core")
    nx, ng = lax.axis_size("x"), lax.axis_size("zg")
    nz = ng * lax.axis_size("zp")
    bound = 2.0 * math.sqrt(D * DO)

    own = acts.reshape(recs * rows, feats)
    full = lax.all_gather(own, tensor, axis=0, tiled=False)
    swap = [(a * nx + b, b * nx + a) for a in range(nx) for b in range(nx)]
    swapped = lax.ppermute(own, ("x", "y"), swap)

    wz = lax.all_gather(weight, ("zg", "zp"), axis=0, tiled=True)
    swapped, wz = lax.optimization_barrier((swapped, wz))
    mine = lax.all_gather(swapped, tensor, axis=0, tiled=False)
    w_blocks = ring_gather(wz)

    vocab_ids = lax.broadcasted_iota(jnp.int32, (1, 1, emb.shape[0]), 2)
    counts = jnp.sum((cond[:, :, None] == vocab_ids).astype(F32), axis=1).astype(BF16)
    bias = jnp.dot(counts, emb, preferred_element_type=F32)
    wrow = jnp.repeat(
        (1.0 / (times + 0.25)).reshape(recs * draws) * (1.0 / math.sqrt(rows)), events
    )[:, None]

    vmem = pl.BlockSpec(memory_space=pltpu.VMEM)
    hbm = pl.BlockSpec(memory_space=pltpu.HBM)
    grads, sq = pl.pallas_call(
        grad_kernel,
        in_specs=[hbm, hbm] + [vmem] * 10,
        out_specs=[vmem, vmem],
        out_shape=[
            jax.ShapeDtypeStruct((recs * rows, local_out), BF16),
            jax.ShapeDtypeStruct((nt, 128), F32),
        ],
        scratch_shapes=[
            pltpu.VMEM((nt, recs * rows, feats), BF16),
            pltpu.VMEM((recs, rows, local_out), BF16),
            pltpu.SemaphoreType.DMA((nt,)),
            pltpu.SemaphoreType.DMA((recs,)),
        ],
        compiler_params=params(51),
        cost_estimate=pl.CostEstimate(
            flops=2 * recs * rows * (local_out + rows) * D,
            bytes_accessed=2 * recs * rows * D + 2 * D * local_out,
            transcendentals=0,
        ),
    )(full, noise_draws.reshape(recs, rows, local_out), bias, wrow, *w_blocks)

    sq_all = lax.all_to_all(sq.reshape(nt, 1, 128), tensor, 0, 0).reshape(nt, 128)
    norms = jnp.sqrt(jnp.sum(sq_all[:, :recs], axis=0))

    packed = pl.pallas_call(
        functools.partial(pack_kernel, bound=bound),
        out_shape=jax.ShapeDtypeStruct((nx, recs * rows + TAIL, local_out), BF16),
        compiler_params=params(),
    )(sq_all, grads)
    packed = lax.all_to_all(packed, "x", 0, 0)
    block = weight.shape[0]
    keep, send = pl.pallas_call(
        functools.partial(sum_kernel, recs=recs),
        in_specs=[hbm, vmem],
        out_specs=[vmem, vmem],
        out_shape=[jax.ShapeDtypeStruct((ng, block, local_out), F32)] * 2,
        scratch_shapes=[
            pltpu.VMEM((nt, recs * rows, feats), BF16),
            pltpu.VMEM((D // nx, local_out), F32),
            pltpu.SemaphoreType.DMA((nt,)),
        ],
        compiler_params=params(51),
        cost_estimate=pl.CostEstimate(
            flops=2 * recs * rows * local_out * D,
            bytes_accessed=2 * recs * rows * (D + nx * local_out) + 4 * D // nx * local_out,
            transcendentals=0,
        ),
    )(mine.reshape(nt, recs * rows, feats), packed)

    got = lax.ppermute(root(send).astype(F16), "zp", [(0, 1), (1, 0)])
    sent = root(keep + unroot(got)).astype(F16)
    clipped_sum = jnp.sum(unroot(lax.all_to_all(sent, "zg", 0, 0)), axis=0)
    total_recs = recs * nx * nz
    update = (clipped_sum + bound * noise) / total_recs
    return (clipped_sum, update, norms)


def solution(mesh):
    grid = Mesh(mesh.devices.reshape(4, 8, 2, 4, 2), ("x", "zg", "zp", "y", "core"))
    dp, tensor = ("x", "zg", "zp"), ("y", "core")
    in_specs = (
        P(dp, None, None, tensor),
        P(dp, None, None, tensor),
        P(dp, None),
        P(dp, None),
        P(None, tensor),
        P(dp, tensor),
        P(dp, tensor),
    )
    out_specs = (P(dp, tensor), P(dp, tensor), P(dp))
    return jax.shard_map(
        on_device, mesh=grid, in_specs=in_specs, out_specs=out_specs, check_vma=False
    )
```

```python
import functools
import math

import jax
import jax.numpy as jnp
from jax import lax
from jax.experimental import pallas as pl
from jax.experimental.pallas import tpu as pltpu
from jax.sharding import Mesh, PartitionSpec as P

D = 4096
DO = 2048
F32 = jnp.float32
BF16 = jnp.bfloat16
F16 = jnp.float16
SCALE = 256.0
MIB = 1024 * 1024


def params(mib=40):
    return pltpu.CompilerParams(vmem_limit_bytes=mib * MIB)


def dot(a, b, ca, cb):
    return lax.dot_general(a, b, (((ca,), (cb,)), ((), ())), preferred_element_type=F32)


def fetch(src, dst, sems, order=None):
    copies = [
        pltpu.make_async_copy(src.at[order[j] if order else j], dst.at[j], sems.at[j])
        for j in range(dst.shape[0])
    ]
    for copy in copies:
        copy.start()
    return copies


def grad_kernel(*refs):
    h_hbm, n_hbm, b_ref, t_ref = refs[:4]
    w_refs, (g_ref, sq_ref, h_buf, n_buf, h_sems, n_sems) = refs[4:-6], refs[-6:]
    total_rows, feats = h_buf.shape[1:]
    recs, rows, _ = n_buf.shape
    nx = len(w_refs) // 2
    here = lax.axis_index("x")
    order = [lax.rem(here + k // 2, nx) * 2 + k % 2 for k in range(2 * nx)]
    h_copies = fetch(h_hbm, h_buf, h_sems, order)
    n_copies = fetch(n_hbm, n_buf, n_sems)
    lane = lax.broadcasted_iota(jnp.int32, sq_ref.shape, 1)
    out = jnp.zeros(sq_ref.shape, F32)
    for r in range(recs):
        at = slice(r * rows, (r + 1) * rows)
        pred, gram = None, None
        for k, w_ref in enumerate(w_refs):
            if r == 0:
                h_copies[k].wait()
            h = h_buf[k, at, :]
            p, q = dot(h, w_ref[...], 1, 0), dot(h, h, 1, 1)
            pred = p if pred is None else pred + p
            gram = q if gram is None else gram + q
        n_copies[r].wait()
        pred = pred + b_ref[r : r + 1, :]
        g = (t_ref[at, :] * (pred - n_buf[r].astype(F32))).astype(BF16)
        g_ref[at, :] = g
        out = jnp.where(lane == r, jnp.sum(gram * dot(g, g, 1, 1)), out)
    sq_ref[...] = out


def sum_kernel(h_hbm, g_ref, sq_ref, keep_ref, send_ref, h_buf, acc, sems, *, recs, bound):
    copies = fetch(h_hbm, h_buf, sems)
    blocks, total_rows, feats = h_buf.shape
    nx = g_ref.shape[0]
    rows = total_rows // recs
    per = blocks // nx
    for x in range(nx):
        clip = bound / jnp.maximum(jnp.sqrt(sq_ref[x, 0:1, :]), bound)
        for j in range(per):
            copies[x * per + j].wait()
            total = None
            for r in range(recs):
                at = slice(r * rows, (r + 1) * rows)
                block = dot(h_buf[x * per + j, at, :], g_ref[x, at, :], 0, 0) * clip[0:1, r : r + 1]
                total = block if total is None else total + block
            out = slice(j * feats, (j + 1) * feats)
            if x == 0:
                acc[out, :] = total
            else:
                acc[out, :] += total
    groups, size, _ = keep_ref.shape
    odd = lax.axis_index("zp")
    for q in range(groups):
        keep_ref[q] = acc[pl.ds(pl.multiple_of((2 * q + odd) * size, size), size), :]
        send_ref[q] = acc[pl.ds(pl.multiple_of((2 * q + 1 - odd) * size, size), size), :]


def root(v):
    return v * lax.rsqrt(jnp.maximum(jnp.abs(v), 1e-30)) * SCALE


def unroot(v):
    v = v.astype(F32)
    return v * jnp.abs(v) * (1.0 / (SCALE * SCALE))


def ring_gather(v):
    up, down = [(i, (i + 1) % 4) for i in range(4)], [(i, (i + 3) % 4) for i in range(4)]
    half = v.shape[0] // 2
    a, b = v[:half], v[half:]
    a3, b1 = lax.ppermute(a, "x", up), lax.ppermute(b, "x", down)
    b3, a1 = lax.ppermute(b, "x", up), lax.ppermute(a, "x", down)
    a2, b2 = lax.ppermute(a3, "x", up), lax.ppermute(b1, "x", down)
    return [a, b, a1, b1, a2, b2, a3, b3]


def on_device(acts, noise_draws, times, cond, emb, weight, noise):
    recs, draws, events, feats = acts.shape
    rows = draws * events
    local_out = weight.shape[1]
    tensor = ("y", "core")
    nt = lax.axis_size("y") * lax.axis_size("core")
    nx, ng = lax.axis_size("x"), lax.axis_size("zg")
    nz = ng * lax.axis_size("zp")
    bound = 2.0 * math.sqrt(D * DO)

    own = acts.reshape(recs * rows, feats)
    full = lax.all_gather(own, tensor, axis=0, tiled=False)
    swap = [(a * nx + b, b * nx + a) for a in range(nx) for b in range(nx)]
    swapped = lax.ppermute(own, ("x", "y"), swap)

    wz = lax.all_gather(weight, ("zg", "zp"), axis=0, tiled=True)
    swapped, wz = lax.optimization_barrier((swapped, wz))
    mine = lax.all_gather(swapped, tensor, axis=0, tiled=False)
    w_blocks = ring_gather(wz)

    vocab_ids = lax.broadcasted_iota(jnp.int32, (1, 1, emb.shape[0]), 2)
    counts = jnp.sum((cond[:, :, None] == vocab_ids).astype(F32), axis=1).astype(BF16)
    bias = jnp.dot(counts, emb, preferred_element_type=F32)
    wrow = jnp.repeat(
        (1.0 / (times + 0.25)).reshape(recs * draws) * (1.0 / math.sqrt(rows)), events
    )[:, None]

    vmem = pl.BlockSpec(memory_space=pltpu.VMEM)
    hbm = pl.BlockSpec(memory_space=pltpu.HBM)
    grads, sq = pl.pallas_call(
        grad_kernel,
        in_specs=[hbm, hbm] + [vmem] * 10,
        out_specs=[vmem, vmem],
        out_shape=[
            jax.ShapeDtypeStruct((recs * rows, local_out), BF16),
            jax.ShapeDtypeStruct((nt, 128), F32),
        ],
        scratch_shapes=[
            pltpu.VMEM((nt, recs * rows, feats), BF16),
            pltpu.VMEM((recs, rows, local_out), BF16),
            pltpu.SemaphoreType.DMA((nt,)),
            pltpu.SemaphoreType.DMA((recs,)),
        ],
        compiler_params=params(51),
        cost_estimate=pl.CostEstimate(
            flops=2 * recs * rows * (local_out + rows) * D,
            bytes_accessed=2 * recs * rows * D + 2 * D * local_out,
            transcendentals=0,
        ),
    )(full, noise_draws.reshape(recs, rows, local_out), bias, wrow, *w_blocks)

    all_grads = lax.all_to_all(
        jnp.broadcast_to(grads[None], (nx, recs * rows, local_out)), "x", 0, 0
    )
    sq = lax.psum(sq + lax.ppermute(sq, "core", [(0, 1), (1, 0)]), "y")
    norms = jnp.sqrt(sq[0, :recs])
    all_sq = lax.all_gather(sq, "x", axis=0, tiled=False)

    block = weight.shape[0]
    keep, send = pl.pallas_call(
        functools.partial(sum_kernel, recs=recs, bound=bound),
        in_specs=[hbm, vmem, vmem],
        out_specs=[vmem, vmem],
        out_shape=[jax.ShapeDtypeStruct((ng, block, local_out), F32)] * 2,
        scratch_shapes=[
            pltpu.VMEM((nt, recs * rows, feats), BF16),
            pltpu.VMEM((D // nx, local_out), F32),
            pltpu.SemaphoreType.DMA((nt,)),
        ],
        compiler_params=params(51),
        cost_estimate=pl.CostEstimate(
            flops=2 * recs * rows * local_out * D,
            bytes_accessed=2 * recs * rows * (D + nx * local_out) + 4 * D // nx * local_out,
            transcendentals=0,
        ),
    )(mine.reshape(nt, recs * rows, feats), all_grads, all_sq)

    got = lax.ppermute(root(send).astype(F16), "zp", [(0, 1), (1, 0)])
    sent = root(keep + unroot(got)).astype(F16)
    clipped_sum = jnp.sum(unroot(lax.all_to_all(sent, "zg", 0, 0)), axis=0)
    total_recs = recs * nx * nz
    update = (clipped_sum + bound * noise) / total_recs
    return (clipped_sum, update, norms)


def solution(mesh):
    grid = Mesh(mesh.devices.reshape(4, 8, 2, 4, 2), ("x", "zg", "zp", "y", "core"))
    dp, tensor = ("x", "zg", "zp"), ("y", "core")
    in_specs = (
        P(dp, None, None, tensor),
        P(dp, None, None, tensor),
        P(dp, None),
        P(dp, None),
        P(None, tensor),
        P(dp, tensor),
        P(dp, tensor),
    )
    out_specs = (P(dp, tensor), P(dp, tensor), P(dp))
    return jax.shard_map(
        on_device, mesh=grid, in_specs=in_specs, out_specs=out_specs, check_vma=False
    )
```

```python
import functools
import math

import jax
import jax.numpy as jnp
from jax import lax
from jax.experimental import pallas as pl
from jax.experimental.pallas import tpu as pltpu
from jax.sharding import Mesh, PartitionSpec as P

D = 4096
DO = 2048
F32 = jnp.float32
BF16 = jnp.bfloat16
F16 = jnp.float16
SCALE = 256.0
AFTER = 6
MIB = 1024 * 1024


def params(mib=40):
    return pltpu.CompilerParams(vmem_limit_bytes=mib * MIB)


def dot(a, b, ca, cb):
    return lax.dot_general(a, b, (((ca,), (cb,)), ((), ())), preferred_element_type=F32)


def fetch(src, dst, sems, order=None):
    copies = [
        pltpu.make_async_copy(src.at[order[j] if order else j], dst.at[j], sems.at[j])
        for j in range(dst.shape[0])
    ]
    for copy in copies:
        copy.start()
    return copies


def gram_kernel(h_hbm, n_hbm, after, h_ref, n_ref, gram_ref, h_sems, n_sems):
    recs, rows, _ = gram_ref.shape
    blocks = h_ref.shape[0]
    nx = blocks // 2
    here = lax.axis_index("x")
    order = [lax.rem(here + k // 2, nx) * 2 + k % 2 for k in range(blocks)]
    h_copies = fetch(h_hbm, h_ref, h_sems, order)
    n_copies = fetch(n_hbm, n_ref, n_sems)
    for r in range(recs):
        total = None
        for k in range(blocks):
            if r == 0:
                h_copies[k].wait()
            h = h_ref[k, r * rows : (r + 1) * rows, :]
            q = dot(h, h, 1, 1)
            total = q if total is None else total + q
        gram_ref[r] = total
    for copy in n_copies:
        copy.wait()


def grad_kernel(*refs):
    h_ref, n_ref, gram_ref, b_ref, t_ref = refs[:5]
    w_refs, (g_ref, sq_ref) = refs[5:-2], refs[-2:]
    recs, rows, _ = gram_ref.shape
    events = rows // t_ref.shape[1]
    row = lax.broadcasted_iota(jnp.int32, sq_ref.shape, 0)
    lane = lax.broadcasted_iota(jnp.int32, sq_ref.shape, 1)
    out = jnp.zeros(sq_ref.shape, F32)
    for r in range(recs):
        at = slice(r * rows, (r + 1) * rows)
        pred = None
        for k, w_ref in enumerate(w_refs):
            p = dot(h_ref[k, at, :], w_ref[...], 1, 0)
            pred = p if pred is None else pred + p
        diff = pred + b_ref[r : r + 1, :] - n_ref[r].astype(F32)
        parts = []
        for a in range(t_ref.shape[1]):
            wgt = 1.0 / (t_ref[r : r + 1, a : a + 1] + 0.25)
            parts.append(wgt * diff[a * events : (a + 1) * events, :])
        g = (jnp.concatenate(parts, axis=0) * (1.0 / math.sqrt(rows))).astype(BF16)
        for k in range(g_ref.shape[0]):
            g_ref[k, at, :] = g
        out = jnp.where(lane == r, jnp.sum(gram_ref[r] * dot(g, g, 1, 1)), out)
    sq_ref[...] = jnp.where(row == lax.axis_index("x"), out, 0.0)


def sum_kernel(h_hbm, g_ref, sq_ref, keep_ref, send_ref, h_buf, acc, sems, *, recs, bound):
    copies = fetch(h_hbm, h_buf, sems)
    blocks, total_rows, feats = h_buf.shape
    nx = g_ref.shape[0]
    rows = total_rows // recs
    per = blocks // nx
    for x in range(nx):
        clip = bound / jnp.maximum(jnp.sqrt(sq_ref[x : x + 1, :]), bound)
        for j in range(per):
            copies[x * per + j].wait()
            total = None
            for r in range(recs):
                at = slice(r * rows, (r + 1) * rows)
                block = dot(h_buf[x * per + j, at, :], g_ref[x, at, :], 0, 0) * clip[0:1, r : r + 1]
                total = block if total is None else total + block
            out = slice(j * feats, (j + 1) * feats)
            if x == 0:
                acc[out, :] = total
            else:
                acc[out, :] += total
    groups, size, _ = keep_ref.shape
    odd = lax.axis_index("zp")
    for q in range(groups):
        keep_ref[q] = acc[pl.ds(pl.multiple_of((2 * q + odd) * size, size), size), :]
        send_ref[q] = acc[pl.ds(pl.multiple_of((2 * q + 1 - odd) * size, size), size), :]


def root(v):
    return v * lax.rsqrt(jnp.maximum(jnp.abs(v), 1e-30)) * SCALE


def unroot(v):
    v = v.astype(F32)
    return v * jnp.abs(v) * (1.0 / (SCALE * SCALE))


def ring_gather(v):
    up, down = [(i, (i + 1) % 4) for i in range(4)], [(i, (i + 3) % 4) for i in range(4)]
    half = v.shape[0] // 2
    a, b = v[:half], v[half:]
    a3, b1 = lax.ppermute(a, "x", up), lax.ppermute(b, "x", down)
    b3, a1 = lax.ppermute(b, "x", up), lax.ppermute(a, "x", down)
    a2, b2 = lax.ppermute(a3, "x", up), lax.ppermute(b1, "x", down)
    return [a, b, a1, b1, a2, b2, a3, b3]


def on_device(acts, noise_draws, times, cond, emb, weight, noise):
    recs, draws, events, feats = acts.shape
    rows = draws * events
    local_out = weight.shape[1]
    tensor = ("y", "core")
    nt = lax.axis_size("y") * lax.axis_size("core")
    nx, ng = lax.axis_size("x"), lax.axis_size("zg")
    nz = ng * lax.axis_size("zp")
    bound = 2.0 * math.sqrt(D * DO)

    own = acts.reshape(recs * rows, feats)
    full = lax.all_gather(own, tensor, axis=0, tiled=False)
    swap = [(a * nx + b, b * nx + a) for a in range(nx) for b in range(nx)]
    swapped = lax.ppermute(own, ("x", "y"), swap)

    wz = lax.all_gather(weight, ("zg", "zp"), axis=0, tiled=True)
    swapped, wz = lax.optimization_barrier((swapped, wz))
    mine = lax.all_gather(swapped, tensor, axis=0, tiled=False)
    w_blocks = ring_gather(wz)

    vocab_ids = lax.broadcasted_iota(jnp.int32, (1, 1, emb.shape[0]), 2)
    counts = jnp.sum((cond[:, :, None] == vocab_ids).astype(F32), axis=1).astype(BF16)
    bias = jnp.dot(counts, emb, preferred_element_type=F32)

    vmem = pl.BlockSpec(memory_space=pltpu.VMEM)
    hbm = pl.BlockSpec(memory_space=pltpu.HBM)
    h, n, gram = pl.pallas_call(
        gram_kernel,
        in_specs=[hbm, hbm, pl.BlockSpec(memory_space=pl.ANY)],
        out_specs=[vmem, vmem, vmem],
        out_shape=[
            jax.ShapeDtypeStruct((nt, recs * rows, feats), BF16),
            jax.ShapeDtypeStruct((recs, rows, local_out), BF16),
            jax.ShapeDtypeStruct((recs, rows, rows), F32),
        ],
        scratch_shapes=[pltpu.SemaphoreType.DMA((nt,)), pltpu.SemaphoreType.DMA((recs,))],
        compiler_params=params(48),
        cost_estimate=pl.CostEstimate(
            flops=2 * recs * rows * rows * D, bytes_accessed=4 * recs * rows * D, transcendentals=0
        ),
    )(full, noise_draws.reshape(recs, rows, local_out), w_blocks[AFTER])
    grads, sq = pl.pallas_call(
        grad_kernel,
        in_specs=[vmem] * 13,
        out_specs=[vmem, vmem],
        out_shape=[
            jax.ShapeDtypeStruct((nx, recs * rows, local_out), BF16),
            jax.ShapeDtypeStruct((8, 128), F32),
        ],
        compiler_params=params(),
        cost_estimate=pl.CostEstimate(
            flops=2 * recs * rows * local_out * D,
            bytes_accessed=2 * recs * rows * D + 2 * D * local_out,
            transcendentals=0,
        ),
    )(h, n, gram, bias, times, *w_blocks)

    all_grads = lax.all_to_all(grads, "x", 0, 0)
    sq = sq + lax.ppermute(sq, "core", [(0, 1), (1, 0)])
    for axis in ("y", "x"):
        for pairs in ((1, 0, 3, 2), (3, 2, 1, 0)):
            sq = sq + lax.ppermute(sq, axis, list(enumerate(pairs)))
    norms = jnp.sqrt(lax.dynamic_index_in_dim(sq, lax.axis_index("x"), 0, False)[:recs])

    block = weight.shape[0]
    keep, send = pl.pallas_call(
        functools.partial(sum_kernel, recs=recs, bound=bound),
        in_specs=[hbm, vmem, vmem],
        out_specs=[vmem, vmem],
        out_shape=[jax.ShapeDtypeStruct((ng, block, local_out), F32)] * 2,
        scratch_shapes=[
            pltpu.VMEM((nt, recs * rows, feats), BF16),
            pltpu.VMEM((D // nx, local_out), F32),
            pltpu.SemaphoreType.DMA((nt,)),
        ],
        compiler_params=params(51),
        cost_estimate=pl.CostEstimate(
            flops=2 * recs * rows * local_out * D,
            bytes_accessed=2 * recs * rows * (D + nx * local_out) + 4 * D // nx * local_out,
            transcendentals=0,
        ),
    )(mine.reshape(nt, recs * rows, feats), all_grads, sq)

    got = lax.ppermute(root(send).astype(F16), "zp", [(0, 1), (1, 0)])
    sent = root(keep + unroot(got)).astype(F16)
    clipped_sum = jnp.sum(unroot(lax.all_to_all(sent, "zg", 0, 0)), axis=0)
    total_recs = recs * nx * nz
    update = (clipped_sum + bound * noise) / total_recs
    return (clipped_sum, update, norms)


def solution(mesh):
    grid = Mesh(mesh.devices.reshape(4, 8, 2, 4, 2), ("x", "zg", "zp", "y", "core"))
    dp, tensor = ("x", "zg", "zp"), ("y", "core")
    in_specs = (
        P(dp, None, None, tensor),
        P(dp, None, None, tensor),
        P(dp, None),
        P(dp, None),
        P(None, tensor),
        P(dp, tensor),
        P(dp, tensor),
    )
    out_specs = (P(dp, tensor), P(dp, tensor), P(dp))
    return jax.shard_map(
        on_device, mesh=grid, in_specs=in_specs, out_specs=out_specs, check_vma=False
    )
```

```python
import functools
import math

import jax
import jax.numpy as jnp
from jax import lax
from jax.experimental import pallas as pl
from jax.experimental.pallas import tpu as pltpu
from jax.sharding import Mesh, PartitionSpec as P

D = 4096
DO = 2048
F32 = jnp.float32
BF16 = jnp.bfloat16
F16 = jnp.float16
SCALE = 256.0
AFTER = 6
TAIL = 16
MIB = 1024 * 1024


def params(mib=40):
    return pltpu.CompilerParams(vmem_limit_bytes=mib * MIB)


def dot(a, b, ca, cb):
    return lax.dot_general(a, b, (((ca,), (cb,)), ((), ())), preferred_element_type=F32)


def fetch(src, dst, sems, order=None):
    copies = [
        pltpu.make_async_copy(src.at[order[j] if order else j], dst.at[j], sems.at[j])
        for j in range(dst.shape[0])
    ]
    for copy in copies:
        copy.start()
    return copies


def gram_kernel(h_hbm, n_hbm, after, h_ref, n_ref, gram_ref, h_sems, n_sems):
    recs, rows, _ = gram_ref.shape
    blocks = h_ref.shape[0]
    nx = blocks // 2
    here = lax.axis_index("x")
    order = [lax.rem(here + k // 2, nx) * 2 + k % 2 for k in range(blocks)]
    h_copies = fetch(h_hbm, h_ref, h_sems, order)
    n_copies = fetch(n_hbm, n_ref, n_sems)
    for r in range(recs):
        total = None
        for k in range(blocks):
            if r == 0:
                h_copies[k].wait()
            h = h_ref[k, r * rows : (r + 1) * rows, :]
            q = dot(h, h, 1, 1)
            total = q if total is None else total + q
        gram_ref[r] = total
    for copy in n_copies:
        copy.wait()


def grad_kernel(*refs):
    h_ref, n_ref, gram_ref, b_ref, t_ref = refs[:5]
    w_refs, (g_ref, sq_ref) = refs[5:-2], refs[-2:]
    recs, rows, _ = gram_ref.shape
    events = rows // t_ref.shape[1]
    lane = lax.broadcasted_iota(jnp.int32, sq_ref.shape, 1)
    out = jnp.zeros(sq_ref.shape, F32)
    for r in range(recs):
        at = slice(r * rows, (r + 1) * rows)
        pred = None
        for k, w_ref in enumerate(w_refs):
            p = dot(h_ref[k, at, :], w_ref[...], 1, 0)
            pred = p if pred is None else pred + p
        diff = pred + b_ref[r : r + 1, :] - n_ref[r].astype(F32)
        parts = []
        for a in range(t_ref.shape[1]):
            wgt = 1.0 / (t_ref[r : r + 1, a : a + 1] + 0.25)
            parts.append(wgt * diff[a * events : (a + 1) * events, :])
        g = (jnp.concatenate(parts, axis=0) * (1.0 / math.sqrt(rows))).astype(BF16)
        g_ref[at, :] = g
        out = jnp.where(lane == r, jnp.sum(gram_ref[r] * dot(g, g, 1, 1)), out)
    sq_ref[...] = out


def pack_kernel(sq_ref, g_ref, o_ref, *, bound):
    rows = g_ref.shape[0]
    norms = jnp.sqrt(jnp.sum(sq_ref[...], axis=0, keepdims=True))
    clip = bound / jnp.maximum(norms, bound)
    high = clip.astype(BF16).astype(F32)
    mid = (clip - high).astype(BF16).astype(F32)
    low = clip - high - mid
    shape = (TAIL, clip.shape[1])
    row = lax.broadcasted_iota(jnp.int32, shape, 0)
    tail = jnp.zeros(shape, F32)
    for k, term in enumerate((high, mid, low)):
        tail = jnp.where(row == k, jnp.broadcast_to(term, shape), tail)
    tail = jnp.concatenate([tail] * (o_ref.shape[2] // clip.shape[1]), axis=1).astype(BF16)
    for k in range(o_ref.shape[0]):
        o_ref[k, 0:rows, :] = g_ref[...]
        o_ref[k, rows : rows + TAIL, :] = tail


def sum_kernel(h_hbm, g_ref, keep_ref, send_ref, h_buf, acc, sems, *, recs):
    copies = fetch(h_hbm, h_buf, sems)
    blocks, total_rows, feats = h_buf.shape
    nx = g_ref.shape[0]
    rows = total_rows // recs
    per = blocks // nx
    for x in range(nx):
        tail = g_ref[x, total_rows : total_rows + TAIL, :].astype(F32)
        clip = jnp.sum(tail, axis=0, keepdims=True)
        for j in range(per):
            copies[x * per + j].wait()
            total = None
            for r in range(recs):
                at = slice(r * rows, (r + 1) * rows)
                block = dot(h_buf[x * per + j, at, :], g_ref[x, at, :], 0, 0) * clip[0:1, r : r + 1]
                total = block if total is None else total + block
            out = slice(j * feats, (j + 1) * feats)
            if x == 0:
                acc[out, :] = total
            else:
                acc[out, :] += total
    groups, size, _ = keep_ref.shape
    odd = lax.axis_index("zp")
    for q in range(groups):
        keep_ref[q] = acc[pl.ds(pl.multiple_of((2 * q + odd) * size, size), size), :]
        send_ref[q] = acc[pl.ds(pl.multiple_of((2 * q + 1 - odd) * size, size), size), :]


def root(v):
    return v * lax.rsqrt(jnp.maximum(jnp.abs(v), 1e-30)) * SCALE


def unroot(v):
    v = v.astype(F32)
    return v * jnp.abs(v) * (1.0 / (SCALE * SCALE))


def ring_gather(v):
    up, down = [(i, (i + 1) % 4) for i in range(4)], [(i, (i + 3) % 4) for i in range(4)]
    half = v.shape[0] // 2
    a, b = v[:half], v[half:]
    a3, b1 = lax.ppermute(a, "x", up), lax.ppermute(b, "x", down)
    b3, a1 = lax.ppermute(b, "x", up), lax.ppermute(a, "x", down)
    a2, b2 = lax.ppermute(a3, "x", up), lax.ppermute(b1, "x", down)
    return [a, b, a1, b1, a2, b2, a3, b3]


def on_device(acts, noise_draws, times, cond, emb, weight, noise):
    recs, draws, events, feats = acts.shape
    rows = draws * events
    local_out = weight.shape[1]
    tensor = ("y", "core")
    nt = lax.axis_size("y") * lax.axis_size("core")
    nx, ng = lax.axis_size("x"), lax.axis_size("zg")
    nz = ng * lax.axis_size("zp")
    bound = 2.0 * math.sqrt(D * DO)

    own = acts.reshape(recs * rows, feats)
    full = lax.all_gather(own, tensor, axis=0, tiled=False)
    swap = [(a * nx + b, b * nx + a) for a in range(nx) for b in range(nx)]
    swapped = lax.ppermute(own, ("x", "y"), swap)

    wz = lax.all_gather(weight, ("zg", "zp"), axis=0, tiled=True)
    swapped, wz = lax.optimization_barrier((swapped, wz))
    mine = lax.all_gather(swapped, tensor, axis=0, tiled=False)
    w_blocks = ring_gather(wz)

    vocab_ids = lax.broadcasted_iota(jnp.int32, (1, 1, emb.shape[0]), 2)
    counts = jnp.sum((cond[:, :, None] == vocab_ids).astype(F32), axis=1).astype(BF16)
    bias = jnp.dot(counts, emb, preferred_element_type=F32)

    vmem = pl.BlockSpec(memory_space=pltpu.VMEM)
    hbm = pl.BlockSpec(memory_space=pltpu.HBM)
    h, n, gram = pl.pallas_call(
        gram_kernel,
        in_specs=[hbm, hbm, pl.BlockSpec(memory_space=pl.ANY)],
        out_specs=[vmem, vmem, vmem],
        out_shape=[
            jax.ShapeDtypeStruct((nt, recs * rows, feats), BF16),
            jax.ShapeDtypeStruct((recs, rows, local_out), BF16),
            jax.ShapeDtypeStruct((recs, rows, rows), F32),
        ],
        scratch_shapes=[pltpu.SemaphoreType.DMA((nt,)), pltpu.SemaphoreType.DMA((recs,))],
        compiler_params=params(48),
        cost_estimate=pl.CostEstimate(
            flops=2 * recs * rows * rows * D, bytes_accessed=4 * recs * rows * D, transcendentals=0
        ),
    )(full, noise_draws.reshape(recs, rows, local_out), w_blocks[AFTER])
    grads, sq = pl.pallas_call(
        grad_kernel,
        in_specs=[vmem] * 13,
        out_specs=[vmem, vmem],
        out_shape=[
            jax.ShapeDtypeStruct((recs * rows, local_out), BF16),
            jax.ShapeDtypeStruct((nt, 128), F32),
        ],
        compiler_params=params(),
        cost_estimate=pl.CostEstimate(
            flops=2 * recs * rows * local_out * D,
            bytes_accessed=2 * recs * rows * D + 2 * D * local_out,
            transcendentals=0,
        ),
    )(h, n, gram, bias, times, *w_blocks)

    sq_all = lax.all_to_all(sq.reshape(nt, 1, 128), tensor, 0, 0).reshape(nt, 128)
    norms = jnp.sqrt(jnp.sum(sq_all[:, :recs], axis=0))

    packed = pl.pallas_call(
        functools.partial(pack_kernel, bound=bound),
        out_shape=jax.ShapeDtypeStruct((nx, recs * rows + TAIL, local_out), BF16),
        compiler_params=params(),
    )(sq_all, grads)
    packed = lax.all_to_all(packed, "x", 0, 0)
    block = weight.shape[0]
    keep, send = pl.pallas_call(
        functools.partial(sum_kernel, recs=recs),
        in_specs=[hbm, vmem],
        out_specs=[vmem, vmem],
        out_shape=[jax.ShapeDtypeStruct((ng, block, local_out), F32)] * 2,
        scratch_shapes=[
            pltpu.VMEM((nt, recs * rows, feats), BF16),
            pltpu.VMEM((D // nx, local_out), F32),
            pltpu.SemaphoreType.DMA((nt,)),
        ],
        compiler_params=params(51),
        cost_estimate=pl.CostEstimate(
            flops=2 * recs * rows * local_out * D,
            bytes_accessed=2 * recs * rows * (D + nx * local_out) + 4 * D // nx * local_out,
            transcendentals=0,
        ),
    )(mine.reshape(nt, recs * rows, feats), packed)

    got = lax.ppermute(root(send).astype(F16), "zp", [(0, 1), (1, 0)])
    sent = root(keep + unroot(got)).astype(F16)
    clipped_sum = jnp.sum(unroot(lax.all_to_all(sent, "zg", 0, 0)), axis=0)
    total_recs = recs * nx * nz
    update = (clipped_sum + bound * noise) / total_recs
    return (clipped_sum, update, norms)


def solution(mesh):
    grid = Mesh(mesh.devices.reshape(4, 8, 2, 4, 2), ("x", "zg", "zp", "y", "core"))
    dp, tensor = ("x", "zg", "zp"), ("y", "core")
    in_specs = (
        P(dp, None, None, tensor),
        P(dp, None, None, tensor),
        P(dp, None),
        P(dp, None),
        P(None, tensor),
        P(dp, tensor),
        P(dp, tensor),
    )
    out_specs = (P(dp, tensor), P(dp, tensor), P(dp))
    return jax.shard_map(
        on_device, mesh=grid, in_specs=in_specs, out_specs=out_specs, check_vma=False
    )
```

```python
import functools
import math

import jax
import jax.numpy as jnp
from jax import lax
from jax.experimental import pallas as pl
from jax.experimental.pallas import tpu as pltpu
from jax.sharding import Mesh, PartitionSpec as P

D = 4096
DO = 2048
F32 = jnp.float32
BF16 = jnp.bfloat16
F16 = jnp.float16
SCALE = 256.0
AFTER = 6
TAIL = 16
MIB = 1024 * 1024


def params(mib=40):
    return pltpu.CompilerParams(vmem_limit_bytes=mib * MIB)


def dot(a, b, ca, cb):
    return lax.dot_general(a, b, (((ca,), (cb,)), ((), ())), preferred_element_type=F32)


def fetch(src, dst, sems, order=None):
    copies = [
        pltpu.make_async_copy(src.at[order[j] if order else j], dst.at[j], sems.at[j])
        for j in range(dst.shape[0])
    ]
    for copy in copies:
        copy.start()
    return copies


def gram_kernel(h_hbm, n_hbm, after, h_ref, n_ref, gram_ref, h_sems, n_sems):
    recs, rows, _ = gram_ref.shape
    blocks = h_ref.shape[0]
    nx = blocks // 2
    here = lax.axis_index("x")
    order = [lax.rem(here + k // 2, nx) * 2 + k % 2 for k in range(blocks)]
    h_copies = fetch(h_hbm, h_ref, h_sems, order)
    n_copies = fetch(n_hbm, n_ref, n_sems)
    for r in range(recs):
        total = None
        for k in range(blocks):
            if r == 0:
                h_copies[k].wait()
            h = h_ref[k, r * rows : (r + 1) * rows, :]
            q = dot(h, h, 1, 1)
            total = q if total is None else total + q
        gram_ref[r] = total
    for copy in n_copies:
        copy.wait()


def grad_kernel(*refs):
    h_ref, n_ref, gram_ref, b_ref, t_ref = refs[:5]
    w_refs, (g_ref, sq_ref) = refs[5:-2], refs[-2:]
    recs, rows, _ = gram_ref.shape
    events = rows // t_ref.shape[1]
    lane = lax.broadcasted_iota(jnp.int32, sq_ref.shape, 1)
    out = jnp.zeros(sq_ref.shape, F32)
    for r in range(recs):
        at = slice(r * rows, (r + 1) * rows)
        pred = None
        for k, w_ref in enumerate(w_refs):
            p = dot(h_ref[k, at, :], w_ref[...], 1, 0)
            pred = p if pred is None else pred + p
        diff = pred + b_ref[r : r + 1, :] - n_ref[r].astype(F32)
        parts = []
        for a in range(t_ref.shape[1]):
            wgt = 1.0 / (t_ref[r : r + 1, a : a + 1] + 0.25)
            parts.append(wgt * diff[a * events : (a + 1) * events, :])
        g = (jnp.concatenate(parts, axis=0) * (1.0 / math.sqrt(rows))).astype(BF16)
        g_ref[at, :] = g
        out = jnp.where(lane == r, jnp.sum(gram_ref[r] * dot(g, g, 1, 1)), out)
    sq_ref[...] = out


def pack_kernel(sq_ref, g_ref, o_ref, *, bound):
    rows = g_ref.shape[0]
    norms = jnp.sqrt(jnp.sum(sq_ref[...], axis=0, keepdims=True))
    clip = bound / jnp.maximum(norms, bound)
    high = clip.astype(BF16).astype(F32)
    mid = (clip - high).astype(BF16).astype(F32)
    low = clip - high - mid
    shape = (TAIL, clip.shape[1])
    row = lax.broadcasted_iota(jnp.int32, shape, 0)
    tail = jnp.zeros(shape, F32)
    for k, term in enumerate((high, mid, low)):
        tail = jnp.where(row == k, jnp.broadcast_to(term, shape), tail)
    tail = jnp.concatenate([tail] * (o_ref.shape[2] // clip.shape[1]), axis=1).astype(BF16)
    for k in range(o_ref.shape[0]):
        o_ref[k, 0:rows, :] = g_ref[...]
        o_ref[k, rows : rows + TAIL, :] = tail


def sum_kernel(h_hbm, g_ref, keep_ref, send_ref, h_buf, acc, sems, *, recs):
    copies = fetch(h_hbm, h_buf, sems)
    blocks, total_rows, feats = h_buf.shape
    nx = g_ref.shape[0]
    rows = total_rows // recs
    per = blocks // nx
    for x in range(nx):
        tail = g_ref[x, total_rows : total_rows + TAIL, :].astype(F32)
        clip = jnp.sum(tail, axis=0, keepdims=True)
        for j in range(per):
            copies[x * per + j].wait()
            total = None
            for r in range(recs):
                at = slice(r * rows, (r + 1) * rows)
                block = dot(h_buf[x * per + j, at, :], g_ref[x, at, :], 0, 0) * clip[0:1, r : r + 1]
                total = block if total is None else total + block
            out = slice(j * feats, (j + 1) * feats)
            if x == 0:
                acc[out, :] = total
            else:
                acc[out, :] += total
    groups, size, _ = keep_ref.shape
    odd = lax.axis_index("zp")
    for q in range(groups):
        keep_ref[q] = acc[pl.ds(pl.multiple_of((2 * q + odd) * size, size), size), :]
        send_ref[q] = acc[pl.ds(pl.multiple_of((2 * q + 1 - odd) * size, size), size), :]


def root(v):
    return v * lax.rsqrt(jnp.maximum(jnp.abs(v), 1e-30)) * SCALE


def unroot(v):
    v = v.astype(F32)
    return v * jnp.abs(v) * (1.0 / (SCALE * SCALE))


def ring_gather(v):
    up, down = [(i, (i + 1) % 4) for i in range(4)], [(i, (i + 3) % 4) for i in range(4)]
    half = v.shape[0] // 2
    a, b = v[:half], v[half:]
    a3, b1 = lax.ppermute(a, "x", up), lax.ppermute(b, "x", down)
    b3, a1 = lax.ppermute(b, "x", up), lax.ppermute(a, "x", down)
    a2, b2 = lax.ppermute(a3, "x", up), lax.ppermute(b1, "x", down)
    return [a, b, a1, b1, a2, b2, a3, b3]


def on_device(acts, noise_draws, times, cond, emb, weight, noise):
    recs, draws, events, feats = acts.shape
    rows = draws * events
    local_out = weight.shape[1]
    tensor = ("y", "core")
    nt = lax.axis_size("y") * lax.axis_size("core")
    nx, ng = lax.axis_size("x"), lax.axis_size("zg")
    nz = ng * lax.axis_size("zp")
    bound = 2.0 * math.sqrt(D * DO)

    own = acts.reshape(recs * rows, feats)
    full = lax.all_gather(own, tensor, axis=0, tiled=False)
    swap = [(a * nx + b, b * nx + a) for a in range(nx) for b in range(nx)]
    swapped = lax.ppermute(own, ("x", "y"), swap)

    other = lax.ppermute(weight, "zp", [(0, 1), (1, 0)])
    odd = lax.axis_index("zp") == 1
    pair = jnp.concatenate([jnp.where(odd, other, weight), jnp.where(odd, weight, other)], axis=0)
    wz = lax.all_gather(pair, "zg", axis=0, tiled=True)
    swapped, wz = lax.optimization_barrier((swapped, wz))
    mine = lax.all_gather(swapped, tensor, axis=0, tiled=False)
    w_blocks = ring_gather(wz)

    vocab_ids = lax.broadcasted_iota(jnp.int32, (1, 1, emb.shape[0]), 2)
    counts = jnp.sum((cond[:, :, None] == vocab_ids).astype(F32), axis=1).astype(BF16)
    bias = jnp.dot(counts, emb, preferred_element_type=F32)

    vmem = pl.BlockSpec(memory_space=pltpu.VMEM)
    hbm = pl.BlockSpec(memory_space=pltpu.HBM)
    h, n, gram = pl.pallas_call(
        gram_kernel,
        in_specs=[hbm, hbm, pl.BlockSpec(memory_space=pl.ANY)],
        out_specs=[vmem, vmem, vmem],
        out_shape=[
            jax.ShapeDtypeStruct((nt, recs * rows, feats), BF16),
            jax.ShapeDtypeStruct((recs, rows, local_out), BF16),
            jax.ShapeDtypeStruct((recs, rows, rows), F32),
        ],
        scratch_shapes=[pltpu.SemaphoreType.DMA((nt,)), pltpu.SemaphoreType.DMA((recs,))],
        compiler_params=params(48),
        cost_estimate=pl.CostEstimate(
            flops=2 * recs * rows * rows * D, bytes_accessed=4 * recs * rows * D, transcendentals=0
        ),
    )(full, noise_draws.reshape(recs, rows, local_out), w_blocks[AFTER])
    grads, sq = pl.pallas_call(
        grad_kernel,
        in_specs=[vmem] * 13,
        out_specs=[vmem, vmem],
        out_shape=[
            jax.ShapeDtypeStruct((recs * rows, local_out), BF16),
            jax.ShapeDtypeStruct((nt, 128), F32),
        ],
        compiler_params=params(),
        cost_estimate=pl.CostEstimate(
            flops=2 * recs * rows * local_out * D,
            bytes_accessed=2 * recs * rows * D + 2 * D * local_out,
            transcendentals=0,
        ),
    )(h, n, gram, bias, times, *w_blocks)

    sq_all = lax.all_to_all(sq.reshape(nt, 1, 128), tensor, 0, 0).reshape(nt, 128)
    norms = jnp.sqrt(jnp.sum(sq_all[:, :recs], axis=0))

    packed = pl.pallas_call(
        functools.partial(pack_kernel, bound=bound),
        out_shape=jax.ShapeDtypeStruct((nx, recs * rows + TAIL, local_out), BF16),
        compiler_params=params(),
    )(sq_all, grads)
    packed = lax.all_to_all(packed, "x", 0, 0)
    block = weight.shape[0]
    keep, send = pl.pallas_call(
        functools.partial(sum_kernel, recs=recs),
        in_specs=[hbm, vmem],
        out_specs=[vmem, vmem],
        out_shape=[jax.ShapeDtypeStruct((ng, block, local_out), F32)] * 2,
        scratch_shapes=[
            pltpu.VMEM((nt, recs * rows, feats), BF16),
            pltpu.VMEM((D // nx, local_out), F32),
            pltpu.SemaphoreType.DMA((nt,)),
        ],
        compiler_params=params(51),
        cost_estimate=pl.CostEstimate(
            flops=2 * recs * rows * local_out * D,
            bytes_accessed=2 * recs * rows * (D + nx * local_out) + 4 * D // nx * local_out,
            transcendentals=0,
        ),
    )(mine.reshape(nt, recs * rows, feats), packed)

    got = lax.ppermute(root(send).astype(F16), "zp", [(0, 1), (1, 0)])
    sent = root(keep + unroot(got)).astype(F16)
    clipped_sum = jnp.sum(unroot(lax.all_to_all(sent, "zg", 0, 0)), axis=0)
    total_recs = recs * nx * nz
    update = (clipped_sum + bound * noise) / total_recs
    return (clipped_sum, update, norms)


def solution(mesh):
    grid = Mesh(mesh.devices.reshape(4, 8, 2, 4, 2), ("x", "zg", "zp", "y", "core"))
    dp, tensor = ("x", "zg", "zp"), ("y", "core")
    in_specs = (
        P(dp, None, None, tensor),
        P(dp, None, None, tensor),
        P(dp, None),
        P(dp, None),
        P(None, tensor),
        P(dp, tensor),
        P(dp, tensor),
    )
    out_specs = (P(dp, tensor), P(dp, tensor), P(dp))
    return jax.shard_map(
        on_device, mesh=grid, in_specs=in_specs, out_specs=out_specs, check_vma=False
    )
```

```python
import functools
import math

import jax
import jax.numpy as jnp
from jax import lax
from jax.experimental import pallas as pl
from jax.experimental.pallas import tpu as pltpu
from jax.sharding import Mesh, PartitionSpec as P

D = 4096
DO = 2048
F32 = jnp.float32
BF16 = jnp.bfloat16
F16 = jnp.float16
SCALE = 256.0
AFTER = 6
TAIL = 16
MIB = 1024 * 1024


def params(mib=40):
    return pltpu.CompilerParams(vmem_limit_bytes=mib * MIB)


def dot(a, b, ca, cb):
    return lax.dot_general(a, b, (((ca,), (cb,)), ((), ())), preferred_element_type=F32)


def fetch(src, dst, sems, order=None):
    copies = [
        pltpu.make_async_copy(src.at[order[j] if order else j], dst.at[j], sems.at[j])
        for j in range(dst.shape[0])
    ]
    for copy in copies:
        copy.start()
    return copies


def gram_kernel(h_hbm, after, h_ref, gram_ref, h_sems):
    recs, rows, _ = gram_ref.shape
    blocks = h_ref.shape[0]
    nx = blocks // 2
    here = lax.axis_index("x")
    order = [lax.rem(here + k // 2, nx) * 2 + k % 2 for k in range(blocks)]
    h_copies = fetch(h_hbm, h_ref, h_sems, order)
    for r in range(recs):
        total = None
        for k in range(blocks):
            if r == 0:
                h_copies[k].wait()
            h = h_ref[k, r * rows : (r + 1) * rows, :]
            q = dot(h, h, 1, 1)
            total = q if total is None else total + q
        gram_ref[r] = total


def grad_kernel(*refs):
    h_ref, n_ref, gram_ref, cond_ref, emb_ref, t_ref = refs[:6]
    w_refs, (g_ref, sq_ref) = refs[6:-2], refs[-2:]
    recs, rows, _ = gram_ref.shape
    events = rows // t_ref.shape[1]
    lane = lax.broadcasted_iota(jnp.int32, sq_ref.shape, 1)
    out = jnp.zeros(sq_ref.shape, F32)
    shape = (8, emb_ref.shape[0])
    ids = lax.broadcasted_iota(jnp.int32, shape, 1)
    owner = lax.broadcasted_iota(jnp.int32, shape, 0)
    counts = jnp.zeros(shape, F32)
    for r in range(recs):
        for k in range(cond_ref.shape[1]):
            counts += jnp.where((owner == r) & (ids == cond_ref[r, k]), 1.0, 0.0)
    bias = dot(counts.astype(BF16), emb_ref[...], 1, 0)
    for r in range(recs):
        at = slice(r * rows, (r + 1) * rows)
        pred = None
        for k, w_ref in enumerate(w_refs):
            p = dot(h_ref[k, at, :], w_ref[...], 1, 0)
            pred = p if pred is None else pred + p
        diff = pred + bias[r : r + 1, :] - n_ref[r].astype(F32)
        parts = []
        for a in range(t_ref.shape[1]):
            wgt = 1.0 / (t_ref[r : r + 1, a : a + 1] + 0.25)
            parts.append(wgt * diff[a * events : (a + 1) * events, :])
        g = (jnp.concatenate(parts, axis=0) * (1.0 / math.sqrt(rows))).astype(BF16)
        g_ref[at, :] = g
        out = jnp.where(lane == r, jnp.sum(gram_ref[r] * dot(g, g, 1, 1)), out)
    sq_ref[...] = out


def pack_kernel(sq_ref, g_ref, o_ref, *, bound):
    rows = g_ref.shape[0]
    norms = jnp.sqrt(jnp.sum(sq_ref[...], axis=0, keepdims=True))
    clip = bound / jnp.maximum(norms, bound)
    high = clip.astype(BF16).astype(F32)
    mid = (clip - high).astype(BF16).astype(F32)
    low = clip - high - mid
    shape = (TAIL, clip.shape[1])
    row = lax.broadcasted_iota(jnp.int32, shape, 0)
    tail = jnp.zeros(shape, F32)
    for k, term in enumerate((high, mid, low)):
        tail = jnp.where(row == k, jnp.broadcast_to(term, shape), tail)
    tail = jnp.concatenate([tail] * (o_ref.shape[2] // clip.shape[1]), axis=1).astype(BF16)
    for k in range(o_ref.shape[0]):
        o_ref[k, 0:rows, :] = g_ref[...]
        o_ref[k, rows : rows + TAIL, :] = tail


def sum_kernel(h_hbm, g_ref, keep_ref, send_ref, h_buf, acc, sems, *, recs):
    copies = fetch(h_hbm, h_buf, sems)
    blocks, total_rows, feats = h_buf.shape
    nx = g_ref.shape[0]
    rows = total_rows // recs
    per = blocks // nx
    for x in range(nx):
        tail = g_ref[x, total_rows : total_rows + TAIL, :].astype(F32)
        clip = jnp.sum(tail, axis=0, keepdims=True)
        for j in range(per):
            copies[x * per + j].wait()
            total = None
            for r in range(recs):
                at = slice(r * rows, (r + 1) * rows)
                block = dot(h_buf[x * per + j, at, :], g_ref[x, at, :], 0, 0) * clip[0:1, r : r + 1]
                total = block if total is None else total + block
            out = slice(j * feats, (j + 1) * feats)
            if x == 0:
                acc[out, :] = total
            else:
                acc[out, :] += total
    groups, size, _ = keep_ref.shape
    odd = lax.axis_index("zp")
    for q in range(groups):
        keep_ref[q] = acc[pl.ds(pl.multiple_of((2 * q + odd) * size, size), size), :]
        send_ref[q] = acc[pl.ds(pl.multiple_of((2 * q + 1 - odd) * size, size), size), :]


def root(v):
    return v * lax.rsqrt(jnp.maximum(jnp.abs(v), 1e-30)) * SCALE


def unroot(v):
    v = v.astype(F32)
    return v * jnp.abs(v) * (1.0 / (SCALE * SCALE))


def ring_gather(v):
    up, down = [(i, (i + 1) % 4) for i in range(4)], [(i, (i + 3) % 4) for i in range(4)]
    half = v.shape[0] // 2
    a, b = v[:half], v[half:]
    a3, b1 = lax.ppermute(a, "x", up), lax.ppermute(b, "x", down)
    b3, a1 = lax.ppermute(b, "x", up), lax.ppermute(a, "x", down)
    a2, b2 = lax.ppermute(a3, "x", up), lax.ppermute(b1, "x", down)
    return [a, b, a1, b1, a2, b2, a3, b3]


def on_device(acts, noise_draws, times, cond, emb, weight, noise):
    recs, draws, events, feats = acts.shape
    rows = draws * events
    local_out = weight.shape[1]
    tensor = ("y", "core")
    nt = lax.axis_size("y") * lax.axis_size("core")
    nx, ng = lax.axis_size("x"), lax.axis_size("zg")
    nz = ng * lax.axis_size("zp")
    bound = 2.0 * math.sqrt(D * DO)

    own = acts.reshape(recs * rows, feats)
    full = lax.all_gather(own, tensor, axis=0, tiled=False)
    swap = [(a * nx + b, b * nx + a) for a in range(nx) for b in range(nx)]
    swapped = lax.ppermute(own, ("x", "y"), swap)

    wz = lax.all_gather(weight, ("zg", "zp"), axis=0, tiled=True)
    swapped, wz = lax.optimization_barrier((swapped, wz))
    mine = lax.all_gather(swapped, tensor, axis=0, tiled=False)
    w_blocks = ring_gather(wz)

    vmem = pl.BlockSpec(memory_space=pltpu.VMEM)
    hbm = pl.BlockSpec(memory_space=pltpu.HBM)
    h, gram = pl.pallas_call(
        gram_kernel,
        in_specs=[hbm, pl.BlockSpec(memory_space=pl.ANY)],
        out_specs=[vmem, vmem],
        out_shape=[
            jax.ShapeDtypeStruct((nt, recs * rows, feats), BF16),
            jax.ShapeDtypeStruct((recs, rows, rows), F32),
        ],
        scratch_shapes=[pltpu.SemaphoreType.DMA((nt,))],
        compiler_params=params(48),
        cost_estimate=pl.CostEstimate(
            flops=2 * recs * rows * rows * D, bytes_accessed=4 * recs * rows * D, transcendentals=0
        ),
    )(full, w_blocks[AFTER])
    grads, sq = pl.pallas_call(
        grad_kernel,
        in_specs=[vmem] * 3 + [pl.BlockSpec(memory_space=pltpu.SMEM)] + [vmem] * 10,
        out_specs=[vmem, vmem],
        out_shape=[
            jax.ShapeDtypeStruct((recs * rows, local_out), BF16),
            jax.ShapeDtypeStruct((nt, 128), F32),
        ],
        compiler_params=params(),
        cost_estimate=pl.CostEstimate(
            flops=2 * recs * rows * local_out * D,
            bytes_accessed=2 * recs * rows * D + 2 * D * local_out,
            transcendentals=0,
        ),
    )(h, noise_draws.reshape(recs, rows, local_out), gram, cond, emb, times, *w_blocks)

    sq_all = lax.all_to_all(sq.reshape(nt, 1, 128), tensor, 0, 0).reshape(nt, 128)
    norms = jnp.sqrt(jnp.sum(sq_all[:, :recs], axis=0))

    packed = pl.pallas_call(
        functools.partial(pack_kernel, bound=bound),
        out_shape=jax.ShapeDtypeStruct((nx, recs * rows + TAIL, local_out), BF16),
        compiler_params=params(),
    )(sq_all, grads)
    packed = lax.all_to_all(packed, "x", 0, 0)
    block = weight.shape[0]
    keep, send = pl.pallas_call(
        functools.partial(sum_kernel, recs=recs),
        in_specs=[hbm, vmem],
        out_specs=[vmem, vmem],
        out_shape=[jax.ShapeDtypeStruct((ng, block, local_out), F32)] * 2,
        scratch_shapes=[
            pltpu.VMEM((nt, recs * rows, feats), BF16),
            pltpu.VMEM((D // nx, local_out), F32),
            pltpu.SemaphoreType.DMA((nt,)),
        ],
        compiler_params=params(51),
        cost_estimate=pl.CostEstimate(
            flops=2 * recs * rows * local_out * D,
            bytes_accessed=2 * recs * rows * (D + nx * local_out) + 4 * D // nx * local_out,
            transcendentals=0,
        ),
    )(mine.reshape(nt, recs * rows, feats), packed)

    got = lax.ppermute(root(send).astype(F16), "zp", [(0, 1), (1, 0)])
    sent = root(keep + unroot(got)).astype(F16)
    clipped_sum = jnp.sum(unroot(lax.all_to_all(sent, "zg", 0, 0)), axis=0)
    total_recs = recs * nx * nz
    update = (clipped_sum + bound * noise) / total_recs
    return (clipped_sum, update, norms)


def solution(mesh):
    grid = Mesh(mesh.devices.reshape(4, 8, 2, 4, 2), ("x", "zg", "zp", "y", "core"))
    dp, tensor = ("x", "zg", "zp"), ("y", "core")
    in_specs = (
        P(dp, None, None, tensor),
        P(dp, None, None, tensor),
        P(dp, None),
        P(dp, None),
        P(None, tensor),
        P(dp, tensor),
        P(dp, tensor),
    )
    out_specs = (P(dp, tensor), P(dp, tensor), P(dp))
    return jax.shard_map(
        on_device, mesh=grid, in_specs=in_specs, out_specs=out_specs, check_vma=False
    )
```

```python
import functools
import math

import jax
import jax.numpy as jnp
from jax import lax
from jax.experimental import pallas as pl
from jax.experimental.pallas import tpu as pltpu
from jax.sharding import Mesh, PartitionSpec as P

D = 4096
DO = 2048
F32 = jnp.float32
BF16 = jnp.bfloat16
F16 = jnp.float16
SCALE = 128.0
AFTER = 6
TAIL = 16
MIB = 1024 * 1024


def params(mib=40):
    return pltpu.CompilerParams(vmem_limit_bytes=mib * MIB)


def dot(a, b, ca, cb):
    return lax.dot_general(a, b, (((ca,), (cb,)), ((), ())), preferred_element_type=F32)


def fetch(src, dst, sems, order=None):
    copies = [
        pltpu.make_async_copy(src.at[order[j] if order else j], dst.at[j], sems.at[j])
        for j in range(dst.shape[0])
    ]
    for copy in copies:
        copy.start()
    return copies


def gram_kernel(h_hbm, after, h_ref, gram_ref, h_sems):
    recs, rows, _ = gram_ref.shape
    blocks = h_ref.shape[0]
    nx = blocks // 2
    here = lax.axis_index("x")
    order = [lax.rem(here + k // 2, nx) * 2 + k % 2 for k in range(blocks)]
    h_copies = fetch(h_hbm, h_ref, h_sems, order)
    for r in range(recs):
        total = None
        for k in range(blocks):
            if r == 0:
                h_copies[k].wait()
            h = h_ref[k, r * rows : (r + 1) * rows, :]
            q = dot(h, h, 1, 1)
            total = q if total is None else total + q
        gram_ref[r] = total


def grad_kernel(*refs):
    h_ref, n_ref, gram_ref, cond_ref, emb_ref, t_ref = refs[:6]
    w_refs, (g_ref, sq_ref) = refs[6:-2], refs[-2:]
    recs, rows, _ = gram_ref.shape
    events = rows // t_ref.shape[1]
    lane = lax.broadcasted_iota(jnp.int32, sq_ref.shape, 1)
    out = jnp.zeros(sq_ref.shape, F32)
    shape = (8, emb_ref.shape[0])
    ids = lax.broadcasted_iota(jnp.int32, shape, 1)
    owner = lax.broadcasted_iota(jnp.int32, shape, 0)
    counts = jnp.zeros(shape, F32)
    for r in range(recs):
        for k in range(cond_ref.shape[1]):
            counts += jnp.where((owner == r) & (ids == cond_ref[r, k]), 1.0, 0.0)
    bias = dot(counts.astype(BF16), emb_ref[...], 1, 0)
    for r in range(recs):
        at = slice(r * rows, (r + 1) * rows)
        pred = None
        for k, w_ref in enumerate(w_refs):
            p = dot(h_ref[k, at, :], w_ref[...], 1, 0)
            pred = p if pred is None else pred + p
        diff = pred + bias[r : r + 1, :] - n_ref[r].astype(F32)
        parts = []
        for a in range(t_ref.shape[1]):
            wgt = 1.0 / (t_ref[r : r + 1, a : a + 1] + 0.25)
            parts.append(wgt * diff[a * events : (a + 1) * events, :])
        g = (jnp.concatenate(parts, axis=0) * (1.0 / math.sqrt(rows))).astype(BF16)
        g_ref[at, :] = g
        out = jnp.where(lane == r, jnp.sum(gram_ref[r] * dot(g, g, 1, 1)), out)
    sq_ref[...] = out


def pack_kernel(sq_ref, g_ref, o_ref, *, bound):
    rows = g_ref.shape[0]
    norms = jnp.sqrt(jnp.sum(sq_ref[...], axis=0, keepdims=True))
    clip = bound / jnp.maximum(norms, bound)
    high = clip.astype(BF16).astype(F32)
    mid = (clip - high).astype(BF16).astype(F32)
    low = clip - high - mid
    shape = (TAIL, clip.shape[1])
    row = lax.broadcasted_iota(jnp.int32, shape, 0)
    tail = jnp.zeros(shape, F32)
    for k, term in enumerate((high, mid, low)):
        tail = jnp.where(row == k, jnp.broadcast_to(term, shape), tail)
    tail = jnp.concatenate([tail] * (o_ref.shape[2] // clip.shape[1]), axis=1).astype(BF16)
    for k in range(o_ref.shape[0]):
        o_ref[k, 0:rows, :] = g_ref[...]
        o_ref[k, rows : rows + TAIL, :] = tail


def sum_kernel(h_hbm, g_ref, keep_ref, send_ref, h_buf, acc, sems, *, recs):
    copies = fetch(h_hbm, h_buf, sems)
    blocks, total_rows, feats = h_buf.shape
    nx = g_ref.shape[0]
    rows = total_rows // recs
    per = blocks // nx
    for x in range(nx):
        tail = g_ref[x, total_rows : total_rows + TAIL, :].astype(F32)
        clip = jnp.sum(tail, axis=0, keepdims=True)
        for j in range(per):
            copies[x * per + j].wait()
            total = None
            for r in range(recs):
                at = slice(r * rows, (r + 1) * rows)
                block = dot(h_buf[x * per + j, at, :], g_ref[x, at, :], 0, 0) * clip[0:1, r : r + 1]
                total = block if total is None else total + block
            out = slice(j * feats, (j + 1) * feats)
            if x == 0:
                acc[out, :] = total
            else:
                acc[out, :] += total
    groups, size, _ = keep_ref.shape
    odd = lax.axis_index("zp")
    for q in range(groups):
        keep_ref[q] = acc[pl.ds(pl.multiple_of((2 * q + odd) * size, size), size), :]
        send_ref[q] = acc[pl.ds(pl.multiple_of((2 * q + 1 - odd) * size, size), size), :]


def root(v):
    return v * lax.rsqrt(jnp.maximum(jnp.abs(v), 1e-30)) * SCALE


def unroot(v):
    v = v.astype(F32)
    return v * jnp.abs(v) * (1.0 / (SCALE * SCALE))


def ring_gather(v):
    up, down = [(i, (i + 1) % 4) for i in range(4)], [(i, (i + 3) % 4) for i in range(4)]
    half = v.shape[0] // 2
    a, b = v[:half], v[half:]
    a3, b1 = lax.ppermute(a, "x", up), lax.ppermute(b, "x", down)
    b3, a1 = lax.ppermute(b, "x", up), lax.ppermute(a, "x", down)
    a2, b2 = lax.ppermute(a3, "x", up), lax.ppermute(b1, "x", down)
    return [a, b, a1, b1, a2, b2, a3, b3]


def on_device(acts, noise_draws, times, cond, emb, weight, noise):
    recs, draws, events, feats = acts.shape
    rows = draws * events
    local_out = weight.shape[1]
    tensor = ("y", "core")
    nt = lax.axis_size("y") * lax.axis_size("core")
    nx, ng = lax.axis_size("x"), lax.axis_size("zg")
    nz = ng * lax.axis_size("zp")
    bound = 2.0 * math.sqrt(D * DO)

    own = acts.reshape(recs * rows, feats)
    full = lax.all_gather(own, tensor, axis=0, tiled=False)
    swap = [(a * nx + b, b * nx + a) for a in range(nx) for b in range(nx)]
    swapped = lax.ppermute(own, ("x", "y"), swap)

    wz = lax.all_gather(weight, ("zg", "zp"), axis=0, tiled=True)
    swapped, wz = lax.optimization_barrier((swapped, wz))
    mine = lax.all_gather(swapped, tensor, axis=0, tiled=False)
    w_blocks = ring_gather(wz)

    vmem = pl.BlockSpec(memory_space=pltpu.VMEM)
    hbm = pl.BlockSpec(memory_space=pltpu.HBM)
    h, gram = pl.pallas_call(
        gram_kernel,
        in_specs=[hbm, pl.BlockSpec(memory_space=pl.ANY)],
        out_specs=[vmem, vmem],
        out_shape=[
            jax.ShapeDtypeStruct((nt, recs * rows, feats), BF16),
            jax.ShapeDtypeStruct((recs, rows, rows), F32),
        ],
        scratch_shapes=[pltpu.SemaphoreType.DMA((nt,))],
        compiler_params=params(48),
        cost_estimate=pl.CostEstimate(
            flops=2 * recs * rows * rows * D, bytes_accessed=4 * recs * rows * D, transcendentals=0
        ),
    )(full, w_blocks[AFTER])
    grads, sq = pl.pallas_call(
        grad_kernel,
        in_specs=[vmem] * 3 + [pl.BlockSpec(memory_space=pltpu.SMEM)] + [vmem] * 10,
        out_specs=[vmem, vmem],
        out_shape=[
            jax.ShapeDtypeStruct((recs * rows, local_out), BF16),
            jax.ShapeDtypeStruct((nt, 128), F32),
        ],
        compiler_params=params(),
        cost_estimate=pl.CostEstimate(
            flops=2 * recs * rows * local_out * D,
            bytes_accessed=2 * recs * rows * D + 2 * D * local_out,
            transcendentals=0,
        ),
    )(h, noise_draws.reshape(recs, rows, local_out), gram, cond, emb, times, *w_blocks)

    sq_all = lax.all_to_all(sq.reshape(nt, 1, 128), tensor, 0, 0).reshape(nt, 128)
    norms = jnp.sqrt(jnp.sum(sq_all[:, :recs], axis=0))

    packed = pl.pallas_call(
        functools.partial(pack_kernel, bound=bound),
        out_shape=jax.ShapeDtypeStruct((nx, recs * rows + TAIL, local_out), BF16),
        compiler_params=params(),
    )(sq_all, grads)
    packed = lax.all_to_all(packed, "x", 0, 0)
    block = weight.shape[0]
    keep, send = pl.pallas_call(
        functools.partial(sum_kernel, recs=recs),
        in_specs=[hbm, vmem],
        out_specs=[vmem, vmem],
        out_shape=[jax.ShapeDtypeStruct((ng, block, local_out), F32)] * 2,
        scratch_shapes=[
            pltpu.VMEM((nt, recs * rows, feats), BF16),
            pltpu.VMEM((D // nx, local_out), F32),
            pltpu.SemaphoreType.DMA((nt,)),
        ],
        compiler_params=params(51),
        cost_estimate=pl.CostEstimate(
            flops=2 * recs * rows * local_out * D,
            bytes_accessed=2 * recs * rows * (D + nx * local_out) + 4 * D // nx * local_out,
            transcendentals=0,
        ),
    )(mine.reshape(nt, recs * rows, feats), packed)

    got = lax.ppermute(root(send).astype(F16), "zp", [(0, 1), (1, 0)])
    sent = root(keep + unroot(got)).astype(F16)
    clipped_sum = jnp.sum(unroot(lax.all_to_all(sent, "zg", 0, 0)), axis=0)
    total_recs = recs * nx * nz
    update = (clipped_sum + bound * noise) / total_recs
    return (clipped_sum, update, norms)


def solution(mesh):
    grid = Mesh(mesh.devices.reshape(4, 8, 2, 4, 2), ("x", "zg", "zp", "y", "core"))
    dp, tensor = ("x", "zg", "zp"), ("y", "core")
    in_specs = (
        P(dp, None, None, tensor),
        P(dp, None, None, tensor),
        P(dp, None),
        P(dp, None),
        P(None, tensor),
        P(dp, tensor),
        P(dp, tensor),
    )
    out_specs = (P(dp, tensor), P(dp, tensor), P(dp))
    return jax.shard_map(
        on_device, mesh=grid, in_specs=in_specs, out_specs=out_specs, check_vma=False
    )
```

```python
import functools
import math

import jax
import jax.numpy as jnp
from jax import lax
from jax.experimental import pallas as pl
from jax.experimental.pallas import tpu as pltpu
from jax.sharding import Mesh, PartitionSpec as P

D = 4096
DO = 2048
F32 = jnp.float32
BF16 = jnp.bfloat16
F16 = jnp.float16
SCALE = 128.0
AFTER = 6
TAIL = 16
MIB = 1024 * 1024


def params(mib=40):
    return pltpu.CompilerParams(vmem_limit_bytes=mib * MIB)


def dot(a, b, ca, cb):
    return lax.dot_general(a, b, (((ca,), (cb,)), ((), ())), preferred_element_type=F32)


def fetch(src, dst, sems, order=None):
    copies = [
        pltpu.make_async_copy(src.at[order[j] if order else j], dst.at[j], sems.at[j])
        for j in range(dst.shape[0])
    ]
    for copy in copies:
        copy.start()
    return copies


def gram_kernel(h_hbm, after, h_ref, gram_ref, h_sems):
    recs, rows, _ = gram_ref.shape
    blocks = h_ref.shape[0]
    nx = blocks // 2
    here = lax.axis_index("x")
    order = [lax.rem(here + k // 2, nx) * 2 + k % 2 for k in range(blocks)]
    h_copies = fetch(h_hbm, h_ref, h_sems, order)
    for r in range(recs):
        total = None
        for k in range(blocks):
            if r == 0:
                h_copies[k].wait()
            h = h_ref[k, r * rows : (r + 1) * rows, :]
            q = dot(h, h, 1, 1)
            total = q if total is None else total + q
        gram_ref[r] = total


def grad_kernel(*refs):
    h_ref, n_ref, gram_ref, cond_ref, emb_ref, t_ref = refs[:6]
    w_refs, (g_ref, sq_ref) = refs[6:-2], refs[-2:]
    recs, rows, _ = gram_ref.shape
    events = rows // t_ref.shape[1]
    lane = lax.broadcasted_iota(jnp.int32, sq_ref.shape, 1)
    out = jnp.zeros(sq_ref.shape, F32)
    shape = (8, emb_ref.shape[0])
    ids = lax.broadcasted_iota(jnp.int32, shape, 1)
    owner = lax.broadcasted_iota(jnp.int32, shape, 0)
    counts = jnp.zeros(shape, F32)
    for r in range(recs):
        for k in range(cond_ref.shape[1]):
            counts += jnp.where((owner == r) & (ids == cond_ref[r, k]), 1.0, 0.0)
    bias = dot(counts.astype(BF16), emb_ref[...], 1, 0)
    for r in range(recs):
        at = slice(r * rows, (r + 1) * rows)
        pred = None
        for k, w_ref in enumerate(w_refs):
            p = dot(h_ref[k, at, :], w_ref[...], 1, 0)
            pred = p if pred is None else pred + p
        diff = pred + bias[r : r + 1, :] - n_ref[r].astype(F32)
        parts = []
        for a in range(t_ref.shape[1]):
            wgt = 1.0 / (t_ref[r : r + 1, a : a + 1] + 0.25)
            parts.append(wgt * diff[a * events : (a + 1) * events, :])
        g = (jnp.concatenate(parts, axis=0) * (1.0 / math.sqrt(rows))).astype(BF16)
        g_ref[at, :] = g
        out = jnp.where(lane == r, jnp.sum(gram_ref[r] * dot(g, g, 1, 1)), out)
    sq_ref[...] = out


def pack_kernel(sq_ref, g_ref, o_ref, *, bound):
    rows = g_ref.shape[0]
    norms = jnp.sqrt(jnp.sum(sq_ref[...], axis=0, keepdims=True))
    clip = bound / jnp.maximum(norms, bound)
    high = clip.astype(BF16).astype(F32)
    mid = (clip - high).astype(BF16).astype(F32)
    low = clip - high - mid
    shape = (TAIL, clip.shape[1])
    row = lax.broadcasted_iota(jnp.int32, shape, 0)
    tail = jnp.zeros(shape, F32)
    for k, term in enumerate((high, mid, low)):
        tail = jnp.where(row == k, jnp.broadcast_to(term, shape), tail)
    tail = jnp.concatenate([tail] * (o_ref.shape[2] // clip.shape[1]), axis=1).astype(BF16)
    for k in range(o_ref.shape[0]):
        o_ref[k, 0:rows, :] = g_ref[...]
        o_ref[k, rows : rows + TAIL, :] = tail


def sum_kernel(h_hbm, g_ref, keep_ref, send_ref, h_buf, acc, sems, *, recs):
    copies = fetch(h_hbm, h_buf, sems)
    blocks, total_rows, feats = h_buf.shape
    nx = g_ref.shape[0]
    rows = total_rows // recs
    per = blocks // nx
    for x in range(nx):
        tail = g_ref[x, total_rows : total_rows + TAIL, :].astype(F32)
        clip = jnp.sum(tail, axis=0, keepdims=True)
        for j in range(per):
            copies[x * per + j].wait()
            total = None
            for r in range(recs):
                at = slice(r * rows, (r + 1) * rows)
                block = dot(h_buf[x * per + j, at, :], g_ref[x, at, :], 0, 0) * clip[0:1, r : r + 1]
                total = block if total is None else total + block
            out = slice(j * feats, (j + 1) * feats)
            if x == 0:
                acc[out, :] = total
            else:
                acc[out, :] += total
    groups, size, _ = keep_ref.shape
    odd = lax.axis_index("zp")
    for q in range(groups):
        keep_ref[q] = acc[pl.ds(pl.multiple_of((2 * q + odd) * size, size), size), :]
        send_ref[q] = acc[pl.ds(pl.multiple_of((2 * q + 1 - odd) * size, size), size), :]


def root(v):
    return v * lax.rsqrt(jnp.maximum(jnp.abs(v), 1e-30)) * SCALE


def unroot(v):
    v = v.astype(F32)
    return v * jnp.abs(v) * (1.0 / (SCALE * SCALE))


def ring_gather(v):
    up, down = [(i, (i + 1) % 4) for i in range(4)], [(i, (i + 3) % 4) for i in range(4)]
    half = v.shape[0] // 2
    a, b = v[:half], v[half:]
    a3, b1 = lax.ppermute(a, "x", up), lax.ppermute(b, "x", down)
    b3, a1 = lax.ppermute(b, "x", up), lax.ppermute(a, "x", down)
    a2, b2 = lax.ppermute(a3, "x", up), lax.ppermute(b1, "x", down)
    return [a, b, a1, b1, a2, b2, a3, b3]


def on_device(acts, noise_draws, times, cond, emb, weight, noise):
    recs, draws, events, feats = acts.shape
    rows = draws * events
    local_out = weight.shape[1]
    tensor = ("y", "core")
    nt = lax.axis_size("y") * lax.axis_size("core")
    nx, ng = lax.axis_size("x"), lax.axis_size("zg")
    nz = ng * lax.axis_size("zp")
    bound = 2.0 * math.sqrt(D * DO)

    own = acts.reshape(recs * rows, feats)
    full = lax.all_gather(own, tensor, axis=0, tiled=False)
    swap = [(a * nx + b, b * nx + a) for a in range(nx) for b in range(nx)]
    swapped = lax.ppermute(own, ("x", "y"), swap)

    wz = lax.all_gather(weight, ("zg", "zp"), axis=0, tiled=True)
    swapped, wz = lax.optimization_barrier((swapped, wz))
    mine = lax.all_gather(swapped, tensor, axis=0, tiled=False)
    w_blocks = ring_gather(wz)

    vmem = pl.BlockSpec(memory_space=pltpu.VMEM)
    hbm = pl.BlockSpec(memory_space=pltpu.HBM)
    h, gram = pl.pallas_call(
        gram_kernel,
        in_specs=[hbm, pl.BlockSpec(memory_space=pl.ANY)],
        out_specs=[vmem, vmem],
        out_shape=[
            jax.ShapeDtypeStruct((nt, recs * rows, feats), BF16),
            jax.ShapeDtypeStruct((recs, rows, rows), F32),
        ],
        scratch_shapes=[pltpu.SemaphoreType.DMA((nt,))],
        compiler_params=params(48),
        cost_estimate=pl.CostEstimate(
            flops=2 * recs * rows * rows * D, bytes_accessed=4 * recs * rows * D, transcendentals=0
        ),
    )(full, w_blocks[AFTER])
    grads, sq = pl.pallas_call(
        grad_kernel,
        in_specs=[vmem] * 3 + [pl.BlockSpec(memory_space=pltpu.SMEM)] + [vmem] * 10,
        out_specs=[vmem, vmem],
        out_shape=[
            jax.ShapeDtypeStruct((recs * rows, local_out), BF16),
            jax.ShapeDtypeStruct((nt, 128), F32),
        ],
        compiler_params=params(),
        cost_estimate=pl.CostEstimate(
            flops=2 * recs * rows * local_out * D,
            bytes_accessed=2 * recs * rows * D + 2 * D * local_out,
            transcendentals=0,
        ),
    )(h, noise_draws.reshape(recs, rows, local_out), gram, cond, emb, times, *w_blocks)

    sq_all = lax.all_to_all(sq.reshape(nt, 1, 128), tensor, 0, 0).reshape(nt, 128)
    norms = jnp.sqrt(jnp.sum(sq_all[:, :recs], axis=0))
    mine, norms = lax.optimization_barrier((mine, norms))

    packed = pl.pallas_call(
        functools.partial(pack_kernel, bound=bound),
        out_shape=jax.ShapeDtypeStruct((nx, recs * rows + TAIL, local_out), BF16),
        compiler_params=params(),
    )(sq_all, grads)
    packed = lax.all_to_all(packed, "x", 0, 0)
    block = weight.shape[0]
    keep, send = pl.pallas_call(
        functools.partial(sum_kernel, recs=recs),
        in_specs=[hbm, vmem],
        out_specs=[vmem, vmem],
        out_shape=[jax.ShapeDtypeStruct((ng, block, local_out), F32)] * 2,
        scratch_shapes=[
            pltpu.VMEM((nt, recs * rows, feats), BF16),
            pltpu.VMEM((D // nx, local_out), F32),
            pltpu.SemaphoreType.DMA((nt,)),
        ],
        compiler_params=params(51),
        cost_estimate=pl.CostEstimate(
            flops=2 * recs * rows * local_out * D,
            bytes_accessed=2 * recs * rows * (D + nx * local_out) + 4 * D // nx * local_out,
            transcendentals=0,
        ),
    )(mine.reshape(nt, recs * rows, feats), packed)

    got = lax.ppermute(root(send).astype(F16), "zp", [(0, 1), (1, 0)])
    sent = root(keep + unroot(got)).astype(F16)
    clipped_sum = jnp.sum(unroot(lax.all_to_all(sent, "zg", 0, 0)), axis=0)
    total_recs = recs * nx * nz
    update = (clipped_sum + bound * noise) / total_recs
    return (clipped_sum, update, norms)


def solution(mesh):
    grid = Mesh(mesh.devices.reshape(4, 8, 2, 4, 2), ("x", "zg", "zp", "y", "core"))
    dp, tensor = ("x", "zg", "zp"), ("y", "core")
    in_specs = (
        P(dp, None, None, tensor),
        P(dp, None, None, tensor),
        P(dp, None),
        P(dp, None),
        P(None, tensor),
        P(dp, tensor),
        P(dp, tensor),
    )
    out_specs = (P(dp, tensor), P(dp, tensor), P(dp))
    return jax.shard_map(
        on_device, mesh=grid, in_specs=in_specs, out_specs=out_specs, check_vma=False
    )
```
